256 devices in a mesh: row: 32 (over y, z), col: 8 (over x, core).
Axes of the slice: x: 4, y: 4, z: 8, core: 2. Of those that a mesh axis runs over, the one named last changes fastest.
Arguments:
- tiles: bfloat16 [256, 192, 128, 128], P(('row', 'col')), may hold values from -4 to 4
- tile_row: int32 [256, 192], P(('row', 'col')), may hold values from 0 to 127
- tile_owner: int32 [256, 192, 1], P(('row', 'col')), may hold values from 0 to 31; in each aligned block of 192 rows (0 to 191, 192 to 383, ..., all dimensions but the last counted through in order) at most 7 rows name the same one
- tile_offset: int32 [256, 192], P(('row', 'col')), may hold values from 0 to 15
- counts: int32 [256], P(('row', 'col')), may hold values from 1 to 192, as said below
- sketch: bfloat16 [524288, 128], P(('col', 'row')), may hold values from -6 to 6
Outputs:
- basis: float32 [524288, 128], P(('row', 'col'))
- gram_factor: float32 [128, 128], replicated
The draws below stay inside these ranges and needn't reach their ends.
Inputs may be any that keep to these rules, and one draw needn't show every extreme that they name: Slots 0 to counts[d] - 1 of list d are live; some list has all 192 slots live. `tile_owner`: among the 192 slots of one list at most 7 name the same value, a bound that some block reaches.
All inputs are finite; a program needn't handle non-finite values.
Results may differ from the reference program's by a relative error of at most 0.0003.
Values may be sent and summed in bfloat16 or wider, within the bound.
No kernel may reach another device: no remote copies, remote signals or barrier semaphores. Data moves between devices by JAX's collectives and lax.ppermute only.
A program may use at most 128 MiB of HBM per device.

```python
import math
import jax
import jax.numpy as jnp
import numpy as np
from jax import lax

TILE = 128
SKETCH = 128
BLOCKS_DEV = 16
SLOTS = 192
ORDER = 524288
DEVICES_ALL = 256
PER_OWNER = 7
N_ROW = 32
N_COL = 8


def draw_tiles(key, part):
    key = jax.random.fold_in(key, 5)
    key_scale, key_base = jax.random.split(key, 2)
    lists = N_ROW * N_COL
    level = jnp.arange(lists, dtype=jnp.float32) / max(lists - 1, 1)
    list_scale = jnp.exp(level * math.log(3.0)) * jnp.exp(jax.random.uniform(key_scale, (lists,), jnp.float32, 0.0, math.log(2.0)))
    base = jnp.clip(jax.random.normal(key_base, (lists, SLOTS, TILE, TILE), jnp.float32), -6.0, 6.0)
    values = base * list_scale[:, None, None, None] / math.sqrt(TILE)
    return jnp.clip(values, -4.0, 4.0).astype(jnp.bfloat16)


def draw_counts(key, part):
    key = jax.random.fold_in(key, 11)
    key_shift, key_cut, key_top = jax.random.split(key, 3)
    lists = N_ROW * N_COL
    shift_amount = jax.random.randint(key_shift, (lists,), 0, 4)
    ceiling = jnp.floor_divide(SLOTS, jnp.left_shift(1, shift_amount))
    cut_amount = jnp.remainder(jax.random.randint(key_cut, (lists,), 0, 1 << 30), ceiling // 2 + 1)
    count_values = jnp.maximum(ceiling - cut_amount, 1)
    busiest = jax.random.randint(key_top, (), 0, lists)
    return jnp.where(jnp.arange(lists) == busiest, SLOTS, count_values).astype(jnp.int32)


def plant(array, own_key, smallest, top_value):
    extent = array.shape
    spot = [jax.random.randint(jax.random.fold_in(own_key, axis), (), 0, extent[axis]) for axis in range(len(extent))]
    array = array.at[tuple(spot)].set(smallest)
    longest = extent.index(max(extent))
    spot[longest] = (spot[longest] + 1) % extent[longest]
    return array.at[tuple(spot)].set(top_value)


def block_scale(key, extent, shards, least, high):
    gain = 1.0
    for position, shards_of in shards:
        steps = jax.random.uniform(jax.random.fold_in(jax.random.fold_in(key, 6), position), (shards_of,), jnp.float32, least / len(shards), high / len(shards))
        gain = gain * jnp.repeat(jnp.exp(steps), extent[position] // shards_of).reshape((-1,) + (1,) * (len(extent) - 1 - position))
    return gain


def routed_block(key, own, number, rows, amount, top, reach, skew):
    order = jax.random.permutation(key, amount)
    crowded, common = portions_of(amount, rows * top, reach, skew, True), portions_of(amount, rows * top, reach, skew, False)
    places = jnp.arange(amount)

    def named(tallies, offset_by):
        used = int((tallies > 0).sum())
        fixed = max(1, used // 4)
        moved = fixed + (places - fixed + offset_by * (used - fixed)) % max(1, amount - fixed)
        return jnp.zeros((amount,), jnp.int32).at[order[jnp.where(places < fixed, places, moved)]].set(jnp.asarray(tallies, jnp.int32))

    tallies = jnp.where(number % 4 == 0, named(crowded, number // 4), named(common, number - number // 4 - 1))
    mixed = jax.random.permutation(jax.random.fold_in(own, 3), amount)
    giver, receiver = mixed[0:amount // 2 * 2:2], mixed[1:amount // 2 * 2:2]
    margin = jnp.minimum(tallies[giver] - 1, reach - tallies[receiver]) // 2
    margin = jnp.where((giver == order[0]) | (receiver == order[0]) | (tallies[receiver] == 0), 0, jnp.maximum(margin, 0))
    moved = jax.random.randint(jax.random.fold_in(own, 4), (amount // 2,), 0, 1 << 20) % (margin + 1)
    tallies = tallies.at[giver].add(-moved).at[receiver].add(moved)
    labels = jnp.searchsorted(jnp.cumsum(tallies), jnp.arange(rows * top), side="right").astype(jnp.int32)
    table = labels.reshape(top, rows).T
    table = table[jax.random.permutation(jax.random.fold_in(own, 1), rows)]
    offset_by = jax.random.randint(jax.random.fold_in(own, 2), (rows, 1), 0, top)
    return jnp.take_along_axis(table, (jnp.arange(top)[None, :] + offset_by) % top, axis=1)


def portions_of(count, total, bound, slope, full):
    weights = [(1 << 20) // math.isqrt(standing ** slope) + 1 for standing in range(1, count + 1)]
    largest = bound if full else min(bound, max(-(-total // count), total * weights[0] // sum(weights)))
    least = 1 if total - largest >= count - 1 else 0
    given, spare = [largest] + [least] * (count - 1), total - largest - least * (count - 1)
    while spare > 0:
        free = [i for i in range(1, count) if given[i] < largest] or [i for i in range(1, count) if given[i] < bound]
        pool, budget = sum([weights[i] for i in free]), spare
        for i in free:
            more = min(bound - given[i], max(1, budget * weights[i] // pool), spare)
            given[i] = given[i] + more
            spare = spare - more
    return np.array(given)


def noise(own_key, extent, width, limit, pieces=(), kind=jnp.bfloat16):
    level = block_scale(own_key, extent, pieces, -0.22, 0.18) if pieces else 1.0
    values = jax.random.normal(own_key, extent, jnp.float32) * width * level
    return jnp.minimum(jnp.maximum(values, -limit), limit).astype(kind)


def setup_inputs(seed: int = 0) -> dict:
    key_list = jax.random.split(jax.random.key(seed), 7)
    tiles = draw_tiles(jax.random.fold_in(key_list[6], 71), 0)
    tile_row = plant(jax.random.randint(key_list[1], (DEVICES_ALL, SLOTS), 0, N_COL * BLOCKS_DEV), jax.random.fold_in(key_list[1], 1), 0, (N_COL * BLOCKS_DEV) - 1).astype(jnp.int32)
    tile_owner_keys = jax.random.split(jax.random.fold_in(key_list[2], 1), DEVICES_ALL * SLOTS // SLOTS)
    tile_owner_turns = jax.random.permutation(jax.random.fold_in(key_list[2], 3), DEVICES_ALL * SLOTS // SLOTS)
    tile_owner = jax.vmap(lambda own, number: routed_block(jax.random.fold_in(key_list[2], 2), own, number, SLOTS, N_ROW, 1, PER_OWNER, 1))(tile_owner_keys, tile_owner_turns).reshape((DEVICES_ALL, SLOTS, 1))
    tile_offset = plant(jax.random.randint(key_list[3], (DEVICES_ALL, SLOTS), 0, BLOCKS_DEV), jax.random.fold_in(key_list[3], 1), 0, BLOCKS_DEV - 1).astype(jnp.int32)
    counts = draw_counts(jax.random.fold_in(key_list[6], 71), 0)
    sketch = noise(key_list[5], (ORDER, SKETCH), 1.0, 6.0, ((0, 256),))
    return dict(tiles=tiles, tile_row=tile_row, tile_owner=tile_owner, tile_offset=tile_offset, counts=counts, sketch=sketch)


def panel_term(tiles_list, rows_list, owners_list, offsets_list, count_list, omega_panel):
    columns = owners_list * BLOCKS_DEV + offsets_list
    omega_blocks = jnp.take(omega_panel, columns, axis=0)
    products = jnp.einsum('stu,suk->stk', tiles_list.astype(jnp.float32), omega_blocks, precision=lax.Precision.HIGHEST)
    is_live = jnp.arange(SLOTS, dtype=jnp.int32) < count_list
    segment_ids = jnp.where(is_live, rows_list, N_COL * BLOCKS_DEV).astype(jnp.int32)
    summed = jax.ops.segment_sum(products, segment_ids, num_segments=N_COL * BLOCKS_DEV + 1)
    return summed[:N_COL * BLOCKS_DEV]

def reference(tiles, tile_row, tile_owner, tile_offset, counts, sketch):
    omega = sketch.astype(jnp.float32).reshape(N_COL, N_ROW * BLOCKS_DEV, TILE, SKETCH)

    def one_panel(row_index):

        def add_list(running, col_index):
            list_index = row_index * N_COL + col_index
            term = panel_term(tiles[list_index], tile_row[list_index], tile_owner[list_index, :, 0], tile_offset[list_index], counts[list_index], omega[col_index])
            return (running + term, None)
        start_panel = jnp.zeros((N_COL * BLOCKS_DEV, TILE, SKETCH), jnp.float32)
        running, _ = lax.scan(add_list, start_panel, jnp.arange(N_COL, dtype=jnp.int32))
        return running
    sampled = lax.map(one_panel, jnp.arange(N_ROW, dtype=jnp.int32)).reshape(ORDER, SKETCH)
    gram = jnp.dot(sampled.T.astype(jnp.float32), sampled.astype(jnp.float32), precision=lax.Precision.HIGHEST, preferred_element_type=jnp.float32) / ORDER
    lower = jnp.linalg.cholesky(gram)
    solved = jax.scipy.linalg.solve_triangular(lower, sampled.T, lower=True)
    return (solved.T, lower.T)
```

```python
import functools

import jax
import jax.numpy as jnp
from jax import lax
from jax.experimental import pallas as pl
from jax.experimental.pallas import tpu as pltpu
from jax.sharding import PartitionSpec as P

GROUP = 8
DEPTH = 4
VMEM = 44 * 1024 * 1024
HIGHEST = lax.Precision.HIGHEST


def encode(value):
    top = jnp.max(jnp.abs(value), axis=0, keepdims=True)
    top = jnp.maximum(top, 1e-28) * 1.0001
    power = jnp.floor(jnp.log2(top)) - 14.0
    scaled = jnp.round(value * jnp.exp2(-power))
    coded = jnp.clip(scaled, -32767.0, 32767.0).astype(jnp.int32).astype(jnp.int16)
    return coded, power


def encode_block(get_tile, coded_ref, side, count):
    powers = jnp.zeros((count, side), jnp.float32)
    which = lax.broadcasted_iota(jnp.int32, (count, side), 0)

    def one(t, powers):
        coded, power = encode(get_tile(t))
        coded_ref[pl.ds(pl.multiple_of(t * side, side), side), :] = coded
        return jnp.where(which == t, power, powers)

    powers = lax.fori_loop(0, count, one, powers, unroll=2)
    coded_ref[pl.ds(count * side, count), :] = powers.astype(jnp.int32).astype(jnp.int16)


def decode_scales(coded_ref, side, count):
    return jnp.exp2(coded_ref[pl.ds(count * side, count), :].astype(jnp.int32).astype(jnp.float32))


def products_kernel(
    columns, rows, meta, tiles, omega, keep, send, tile_buf, omega_buf, total, coded, tile_sem, omega_sem, keep_sem, send_sem
):
    groups = meta[0]
    core = meta[1]
    side = tiles.shape[1]
    halves = keep.shape[0]
    blocks = (total.shape[0] - 1) // (2 * halves)

    def fetch(group):
        slot = lax.rem(group, DEPTH)
        first = group * GROUP
        pltpu.make_async_copy(tiles.at[pl.ds(first, GROUP)], tile_buf.at[slot], tile_sem.at[slot]).start()
        for i in range(GROUP):
            pltpu.make_async_copy(
                omega.at[columns[first + i]], omega_buf.at[slot, i], omega_sem.at[slot]
            ).start()

    for g in range(DEPTH - 1):
        @pl.when(g < groups)
        def _():
            fetch(g)

    def clear(t, _):
        total[t] = jnp.zeros(total.shape[1:], jnp.float32)
        return 0

    lax.fori_loop(0, total.shape[0], clear, 0)

    def step(group, _):
        @pl.when(group + (DEPTH - 1) < groups)
        def _():
            fetch(group + (DEPTH - 1))

        slot = lax.rem(group, DEPTH)
        pltpu.make_async_copy(tiles.at[pl.ds(0, GROUP)], tile_buf.at[slot], tile_sem.at[slot]).wait()
        pltpu.make_async_copy(omega.at[pl.ds(0, GROUP)], omega_buf.at[slot], omega_sem.at[slot]).wait()
        parts = [
            jnp.dot(tile_buf[slot, i], omega_buf[slot, i], preferred_element_type=jnp.float32)
            for i in range(GROUP)
        ]
        for i in range(GROUP):
            row = rows[group * GROUP + i]
            total[row] += parts[i]
        return 0

    lax.fori_loop(0, groups, step, 0)

    def keep_copy(x):
        return pltpu.make_async_copy(
            total.at[pl.ds((2 * x + core) * blocks, blocks)], keep.at[x], keep_sem.at[x]
        )

    def send_copy(x):
        return pltpu.make_async_copy(coded.at[x], send.at[x], send_sem.at[x])

    for x in range(halves):
        keep_copy(x).start()
    for x in range(halves):
        first = (2 * x + 1 - core) * blocks
        encode_block(lambda t: total[first + t], coded.at[x], side, blocks)
        send_copy(x).start()
    for x in range(halves):
        keep_copy(x).wait()
        send_copy(x).wait()


def products(tiles, omega, columns, rows, meta, halves):
    slots, side, _ = tiles.shape
    width = omega.shape[2]
    blocks = 16
    panel = 2 * halves * blocks
    any_spec = pl.BlockSpec(memory_space=pl.ANY)
    return pl.pallas_call(
        products_kernel,
        out_shape=(
            jax.ShapeDtypeStruct((halves, blocks, side, width), jnp.float32),
            jax.ShapeDtypeStruct((halves, blocks * side + blocks, width), jnp.int16),
        ),
        grid_spec=pltpu.PrefetchScalarGridSpec(
            num_scalar_prefetch=3,
            grid=(1,),
            in_specs=[any_spec, any_spec],
            out_specs=(any_spec, any_spec),
            scratch_shapes=[
                pltpu.VMEM((DEPTH, GROUP, side, side), jnp.bfloat16),
                pltpu.VMEM((DEPTH, GROUP, side, width), jnp.bfloat16),
                pltpu.VMEM((panel + 1, side, width), jnp.float32),
                pltpu.VMEM((halves, blocks * side + blocks, width), jnp.int16),
                pltpu.SemaphoreType.DMA((DEPTH,)),
                pltpu.SemaphoreType.DMA((DEPTH,)),
                pltpu.SemaphoreType.DMA((halves,)),
                pltpu.SemaphoreType.DMA((halves,)),
            ],
        ),
        compiler_params=pltpu.CompilerParams(vmem_limit_bytes=VMEM),
        cost_estimate=pl.CostEstimate(flops=2 * slots * side**3, bytes_accessed=24 << 20, transcendentals=0),
        name="products",
    )(columns, rows, meta, tiles, omega)


def half_sum_kernel(index, keep, received, coded):
    blocks, side = keep.shape[1:3]
    scales = decode_scales(received.at[0], side, blocks)
    which = lax.broadcasted_iota(jnp.int32, scales.shape, 0)

    def tile(t):
        scale = jnp.sum(jnp.where(which == t, scales, 0.0), axis=0, keepdims=True)
        rows = received[0, pl.ds(pl.multiple_of(t * side, side), side), :]
        return keep[0, t] + rows.astype(jnp.int32).astype(jnp.float32) * scale

    encode_block(tile, coded, side, blocks)


def half_sum(index, keep, received):
    _, blocks, side, width = keep.shape
    length = received.shape[1]
    return pl.pallas_call(
        half_sum_kernel,
        out_shape=jax.ShapeDtypeStruct((length, width), jnp.int16),
        grid_spec=pltpu.PrefetchScalarGridSpec(
            num_scalar_prefetch=1,
            grid=(1,),
            in_specs=[
                pl.BlockSpec((1, blocks, side, width), lambda i, index: (index[0], 0, 0, 0)),
                pl.BlockSpec((1, length, width), lambda i, index: (index[0], 0, 0)),
            ],
            out_specs=pl.BlockSpec((length, width), lambda i, index: (0, 0)),
        ),
        compiler_params=pltpu.CompilerParams(vmem_limit_bytes=VMEM),
        cost_estimate=pl.CostEstimate(flops=1 << 22, bytes_accessed=2 << 20, transcendentals=0),
        name="half_sum",
    )(index, keep, received)


def total_kernel(index, keep, received, first, second, third, sampled, gram):
    blocks, side = keep.shape[1:3]
    parts = [received.at[0], first, second, third]
    scales = [decode_scales(p, side, blocks) for p in parts]
    which = lax.broadcasted_iota(jnp.int32, scales[0].shape, 0)

    def tile(t, _):
        rows = pl.ds(pl.multiple_of(t * side, side), side)
        terms = [keep[0, t]]
        for p, s in zip(parts, scales):
            scale = jnp.sum(jnp.where(which == t, s, 0.0), axis=0, keepdims=True)
            terms.append(p[rows, :].astype(jnp.int32).astype(jnp.float32) * scale)
        sampled[rows, :] = (terms[0] + terms[1]) + (terms[2] + terms[3]) + terms[4]
        return 0

    lax.fori_loop(0, blocks, tile, 0)
    piece = 4 * side
    acc = None
    for i in range(blocks // 4):
        part = sampled[pl.ds(i * piece, piece), :]
        term = lax.dot_general(
            part, part, (((0,), (0,)), ((), ())), precision=HIGHEST, preferred_element_type=jnp.float32
        )
        acc = term if acc is None else acc + term
    gram[...] = acc


def total_sum(index, keep, received, others):
    _, blocks, side, width = keep.shape
    length = received.shape[1]
    whole = pl.BlockSpec((length, width), lambda i, index: (0, 0))
    return pl.pallas_call(
        total_kernel,
        out_shape=(
            jax.ShapeDtypeStruct((blocks * side, width), jnp.float32),
            jax.ShapeDtypeStruct((width, width), jnp.float32),
        ),
        grid_spec=pltpu.PrefetchScalarGridSpec(
            num_scalar_prefetch=1,
            grid=(1,),
            in_specs=[
                pl.BlockSpec((1, blocks, side, width), lambda i, index: (index[0], 0, 0, 0)),
                pl.BlockSpec((1, length, width), lambda i, index: (index[0], 0, 0)),
                whole,
                whole,
                whole,
            ],
            out_specs=(
                pl.BlockSpec((blocks * side, width), lambda i, index: (0, 0)),
                pl.BlockSpec((width, width), lambda i, index: (0, 0)),
            ),
        ),
        compiler_params=pltpu.CompilerParams(vmem_limit_bytes=VMEM),
        name="total_sum",
    )(index, keep, received, *others)


def swap(value, axes, mask, size):
    return lax.ppermute(value, axes, [(i, i ^ mask) for i in range(size)])


def sum_four(value, axes, low, high, size):
    others = [swap(value, axes, m, size) for m in (low, high, low ^ high)]
    return (value + others[0]) + (others[1] + others[2])


def shards(tiles, tile_row, tile_owner, tile_offset, counts, sketch):
    row_count = lax.axis_size("row")
    col_count = lax.axis_size("col")
    slot_count, side = tiles.shape[1:3]
    width = sketch.shape[1]
    blocks = sketch.shape[0] // side
    place = lax.axis_index("col")
    core, chip = place % 2, place // 2
    live = counts[0]
    rows = jnp.where(jnp.arange(slot_count, dtype=jnp.int32) < live, tile_row[0], col_count * blocks)
    columns = tile_owner[0, :, 0] * blocks + tile_offset[0]
    meta = jnp.stack([(live + GROUP - 1) // GROUP, core]).astype(jnp.int32)

    omega = lax.all_gather(sketch, "row", axis=0, tiled=True)
    omega = omega.reshape(row_count * blocks, side, width)
    keep, send = products(tiles[0], omega, columns, rows, meta, col_count // 2)

    received = swap(send, "col", 1, col_count)
    others = []
    for k in (2, 1, 3):
        coded = half_sum((chip ^ k).reshape(1), keep, received)
        others.append(swap(coded, "col", 2 * k, col_count))
    sampled, local_gram = total_sum(chip.reshape(1), keep, received, others)

    both = ("row", "col")
    devices = row_count * col_count
    gram = sum_four(local_gram, both, 1, 4 * col_count, devices)
    gram = sum_four(gram, both, 2, 4, devices)
    gram = sum_four(gram, both, col_count, 2 * col_count, devices)
    gram = sum_four(gram, both, 8 * col_count, 16 * col_count, devices)
    gram = gram / (sampled.shape[0] * devices)
    lower = jnp.linalg.cholesky(gram)
    solved = jax.scipy.linalg.solve_triangular(lower, sampled.T, lower=True)
    return (solved.T, lower.T)


def solution(mesh):
    in_specs = (
        P(("row", "col"), None, None, None),
        P(("row", "col"), None),
        P(("row", "col"), None, None),
        P(("row", "col"), None),
        P(("row", "col")),
        P(("col", "row"), None),
    )
    out_specs = (P(("row", "col"), None), P())
    return jax.shard_map(shards, mesh=mesh, in_specs=in_specs, out_specs=out_specs, check_vma=False)
```

```python
import jax
import jax.numpy as jnp
import numpy as np
from jax import lax
from jax.experimental import pallas as pl
from jax.experimental.pallas import tpu as pltpu
from jax.sharding import PartitionSpec as P

GROUP = 8
VMEM = 60 * 1024 * 1024
Y_SIZE = 4
Z_SIZE = 8
FIRST_SHARE = 10
HIGHEST = lax.Precision.HIGHEST


def encode(value):
    top = jnp.max(jnp.abs(value), axis=0, keepdims=True)
    top = jnp.maximum(top, 1e-28) * 1.0001
    power = jnp.floor(jnp.log2(top)) - 14.0
    scaled = jnp.round(value * jnp.exp2(-power))
    coded = jnp.clip(scaled, -32767.0, 32767.0).astype(jnp.int32).astype(jnp.int16)
    return coded, power


def encode_block(get_tile, coded_ref, side, count):
    powers = jnp.zeros((count, side), jnp.float32)
    which = lax.broadcasted_iota(jnp.int32, (count, side), 0)

    def one(t, powers):
        coded, power = encode(get_tile(t))
        coded_ref[pl.ds(pl.multiple_of(t * side, side), side), :] = coded
        return jnp.where(which == t, power, powers)

    powers = lax.fori_loop(0, count, one, powers, unroll=2)
    coded_ref[pl.ds(count * side, count), :] = powers.astype(jnp.int32).astype(jnp.int16)


def decode_scales(coded_ref, side, count):
    return jnp.exp2(coded_ref[pl.ds(count * side, count), :].astype(jnp.int32).astype(jnp.float32))


class Piece:
    def __init__(self, array, runs):
        self.array = array
        self.runs = runs

    @property
    def blocks(self):
        return sum(run[3] for run in self.runs)


def cut(piece, first, count, side):
    runs, at = [], 0
    for y, z, start, blocks in piece.runs:
        low, high = max(first, at), min(first + count, at + blocks)
        if high > low:
            runs.append((y, z, start + low - at, high - low))
        at += blocks
    return Piece(piece.array[first * side : (first + count) * side], runs)


def join(pieces):
    return Piece(jnp.concatenate([p.array for p in pieces], 0), [r for p in pieces for r in p.runs])


def shift(piece, dy, dz, after=()):
    array = piece.array
    if after:
        array = lax.optimization_barrier((array,) + tuple(p.array for p in after))[0]
    pairs = [
        (y * Z_SIZE + z, (y + dy) % Y_SIZE * Z_SIZE + (z + dz) % Z_SIZE)
        for y in range(Y_SIZE)
        for z in range(Z_SIZE)
    ]
    runs = [((y - dy) % Y_SIZE, (z - dz) % Z_SIZE, start, n) for y, z, start, n in piece.runs]
    return Piece(lax.ppermute(array, "row", pairs), runs)


def gather_rows(sketch, side):
    def both_y(up, down, after=()):
        return shift(up, 1, 0, after), shift(down, -1, 0, after)

    def both_z(up, down, after=()):
        return shift(up, 0, 1, after), shift(down, 0, -1, after)

    def halves(pair):
        half = pair[0].blocks // 2
        return cut(pair[0], 0, half, side), cut(pair[1], half, pair[1].blocks - half, side)

    blocks = sketch.shape[0] // side
    a = Piece(sketch[: FIRST_SHARE * side], [(0, 0, 0, FIRST_SHARE)])
    b = Piece(sketch[FIRST_SHARE * side :], [(0, 0, FIRST_SHARE, blocks - FIRST_SHARE)])
    yb = both_y(b, b)
    za1 = both_z(a, a)
    ya = both_y(a, a)
    yb2 = both_y(*halves(yb))
    za2 = both_z(*za1)
    ya2 = both_y(*halves(ya), after=yb)
    b1, b2 = join([b, yb[0]]), join([yb[1], *yb2])
    za3 = both_z(*za2)
    p1, p2, p3 = join(za1), join(za2), join(za3)
    y1 = both_y(p1, p1, after=yb2)
    z4 = both_z(*halves(za3))
    zb1 = both_z(b1, b1, after=za3)
    y2 = both_y(p2, p2, after=ya2)
    zc1 = both_z(b2, b2, after=z4)
    y12 = both_y(*halves(y1), after=y1)
    zb2 = both_z(*zb1)
    y3 = both_y(p3, p3, after=y2)
    zc2 = both_z(*zc1)
    y22 = both_y(*halves(y2), after=y12)
    zb3 = both_z(*zb2)
    p4 = join(z4)
    y4 = both_y(p4, p4, after=y3)
    zc3 = both_z(*zc2)
    y32 = both_y(*halves(y3), after=y22)
    zb4 = both_z(*halves(zb3))
    zc4 = both_z(*halves(zc3))
    y42 = both_y(*halves(y4), after=y4)
    pieces = [a, *ya, *ya2, p1, *y1, *y12, p2, *y2, *y22, p3, *y3, *y32, p4, *y4, *y42]
    pieces += [b1, b2, *zb1, *zc1, *zb2, *zc2, *zb3, *zc3, *zb4, *zc4]
    table = np.full((Y_SIZE * Z_SIZE * blocks, 2), -1, np.int32)
    for number, piece in enumerate(pieces):
        at = 0
        for y, z, start, count in piece.runs:
            for i in range(count):
                table[(y * Z_SIZE + z) * blocks + start + i] = (number, at)
                at += 1
    assert (table >= 0).all() and sum(p.blocks for p in pieces) == len(table)
    arrays = [p.array.reshape(p.blocks, side, sketch.shape[1]) for p in pieces]
    return arrays, table, yb[0].array


def products_kernel(count, order, starts, place, rows, meta, tiles, *refs):
    omega, (keep, send, tile_buf, omega_buf, total, coded) = refs[:count], refs[count : count + 6]
    tile_sem, omega_sem, keep_sem, send_sem = refs[count + 6 :]
    groups = meta[0]
    core = meta[1]
    side = tiles.shape[1]
    halves = keep.shape[0]
    blocks = (total.shape[0] - 1) // (2 * halves)

    def tile_copy(group):
        part = pl.ds(group * GROUP, GROUP)
        return pltpu.make_async_copy(tiles.at[part], tile_buf.at[part], tile_sem.at[group])

    def fetch_tiles(group, _):
        tile_copy(group).start()
        return 0

    lax.fori_loop(0, groups, fetch_tiles, 0)
    for p in range(count):

        def fetch(j, _, p=p):
            slot = order[j]
            pltpu.make_async_copy(
                omega[p].at[place[slot]], omega_buf.at[slot], omega_sem.at[slot // GROUP]
            ).start()
            return 0

        lax.fori_loop(starts[p], starts[p + 1], fetch, 0)

    def clear(t, _):
        total[t] = jnp.zeros(total.shape[1:], jnp.float32)
        return 0

    lax.fori_loop(0, total.shape[0], clear, 0)

    def step(group, _):
        first = group * GROUP
        tile_copy(group).wait()
        pltpu.make_async_copy(
            tiles.at[pl.ds(0, GROUP)], omega_buf.at[pl.ds(first, GROUP)], omega_sem.at[group]
        ).wait()
        parts = [
            jnp.dot(tile_buf[first + i], omega_buf[first + i], preferred_element_type=jnp.float32)
            for i in range(GROUP)
        ]
        for i in range(GROUP):
            total[rows[first + i]] += parts[i]
        return 0

    lax.fori_loop(0, groups, step, 0)

    def keep_copy(x):
        return pltpu.make_async_copy(
            total.at[pl.ds((2 * x + core) * blocks, blocks)], keep.at[x], keep_sem.at[x]
        )

    def send_copy(x):
        return pltpu.make_async_copy(coded.at[x], send.at[x], send_sem.at[x])

    for x in range(halves):
        keep_copy(x).start()
    for x in range(halves):
        first = (2 * x + 1 - core) * blocks
        encode_block(lambda t: total[first + t], coded.at[x], side, blocks)
        send_copy(x).start()
    for x in range(halves):
        keep_copy(x).wait()
        send_copy(x).wait()


def products(tiles, omega, order, starts, place, rows, meta, halves, blocks):
    slots, side, _ = tiles.shape
    width = omega[0].shape[2]
    panel = 2 * halves * blocks
    any_spec = pl.BlockSpec(memory_space=pl.ANY)
    return pl.pallas_call(
        lambda *refs: products_kernel(len(omega), *refs),
        out_shape=(
            jax.ShapeDtypeStruct((halves, blocks, side, width), jnp.float32),
            jax.ShapeDtypeStruct((halves, blocks * side + blocks, width), jnp.int16),
        ),
        grid_spec=pltpu.PrefetchScalarGridSpec(
            num_scalar_prefetch=5,
            grid=(1,),
            in_specs=[any_spec] * (1 + len(omega)),
            out_specs=(any_spec, any_spec),
            scratch_shapes=[
                pltpu.VMEM((slots, side, side), jnp.bfloat16),
                pltpu.VMEM((slots, side, width), jnp.bfloat16),
                pltpu.VMEM((panel + 1, side, width), jnp.float32),
                pltpu.VMEM((halves, blocks * side + blocks, width), jnp.int16),
                pltpu.SemaphoreType.DMA((slots // GROUP,)),
                pltpu.SemaphoreType.DMA((slots // GROUP,)),
                pltpu.SemaphoreType.DMA((halves,)),
                pltpu.SemaphoreType.DMA((halves,)),
            ],
        ),
        compiler_params=pltpu.CompilerParams(vmem_limit_bytes=VMEM),
        cost_estimate=pl.CostEstimate(flops=2 * slots * side**3, bytes_accessed=24 << 20, transcendentals=0),
        name="products",
    )(order, starts, place, rows, meta, tiles, *omega)


def plan(owner, offset, live, table, pieces, blocks):
    slots = owner.shape[0]
    here = lax.axis_index("row")
    y = (owner // Z_SIZE - here // Z_SIZE) % Y_SIZE
    z = (owner % Z_SIZE - here % Z_SIZE) % Z_SIZE
    code = (y * Z_SIZE + z) * blocks + offset
    chosen = code[:, None] == jnp.arange(len(table), dtype=jnp.int32)[None, :]
    piece = jnp.sum(jnp.where(chosen, jnp.asarray(table[:, 0])[None, :], 0), 1)
    place = jnp.sum(jnp.where(chosen, jnp.asarray(table[:, 1])[None, :], 0), 1)
    groups = (live + GROUP - 1) // GROUP
    number = jnp.arange(slots, dtype=jnp.int32)
    key = jnp.where(number < groups * GROUP, piece, pieces)
    key = key * slots + number
    rank = jnp.sum((key[None, :] < key[:, None]).astype(jnp.int32), 1)
    order = jnp.sum(jnp.where(rank[None, :] == number[:, None], number[None, :], 0), 1)
    limits = jnp.arange(pieces + 1, dtype=jnp.int32) * slots
    starts = jnp.sum((key[None, :] < limits[:, None]).astype(jnp.int32), 1)
    return order, starts, place, groups


def half_sum_kernel(index, keep, received, coded):
    blocks, side = keep.shape[1:3]
    scales = decode_scales(received.at[0], side, blocks)
    which = lax.broadcasted_iota(jnp.int32, scales.shape, 0)

    def tile(t):
        scale = jnp.sum(jnp.where(which == t, scales, 0.0), axis=0, keepdims=True)
        rows = received[0, pl.ds(pl.multiple_of(t * side, side), side), :]
        return keep[0, t] + rows.astype(jnp.int32).astype(jnp.float32) * scale

    encode_block(tile, coded, side, blocks)


def half_sum(index, keep, received):
    _, blocks, side, width = keep.shape
    length = received.shape[1]
    return pl.pallas_call(
        half_sum_kernel,
        out_shape=jax.ShapeDtypeStruct((length, width), jnp.int16),
        grid_spec=pltpu.PrefetchScalarGridSpec(
            num_scalar_prefetch=1,
            grid=(1,),
            in_specs=[
                pl.BlockSpec((1, blocks, side, width), lambda i, index: (index[0], 0, 0, 0)),
                pl.BlockSpec((1, length, width), lambda i, index: (index[0], 0, 0)),
            ],
            out_specs=pl.BlockSpec((length, width), lambda i, index: (0, 0)),
        ),
        compiler_params=pltpu.CompilerParams(vmem_limit_bytes=VMEM),
        cost_estimate=pl.CostEstimate(flops=1 << 22, bytes_accessed=2 << 20, transcendentals=0),
        name="half_sum",
    )(index, keep, received)


def total_kernel(index, keep, received, first, second, third, sampled, gram):
    blocks, side = keep.shape[1:3]
    parts = [received.at[0], first, second, third]
    scales = [decode_scales(p, side, blocks) for p in parts]
    which = lax.broadcasted_iota(jnp.int32, scales[0].shape, 0)

    def tile(t, _):
        rows = pl.ds(pl.multiple_of(t * side, side), side)
        terms = [keep[0, t]]
        for p, s in zip(parts, scales):
            scale = jnp.sum(jnp.where(which == t, s, 0.0), axis=0, keepdims=True)
            terms.append(p[rows, :].astype(jnp.int32).astype(jnp.float32) * scale)
        sampled[rows, :] = (terms[0] + terms[1]) + (terms[2] + terms[3]) + terms[4]
        return 0

    lax.fori_loop(0, blocks, tile, 0)
    piece = 4 * side
    acc = None
    for i in range(blocks // 4):
        part = sampled[pl.ds(i * piece, piece), :]
        term = lax.dot_general(
            part, part, (((0,), (0,)), ((), ())), precision=HIGHEST, preferred_element_type=jnp.float32
        )
        acc = term if acc is None else acc + term
    gram[...] = acc


def total_sum(index, keep, received, others):
    _, blocks, side, width = keep.shape
    length = received.shape[1]
    whole = pl.BlockSpec((length, width), lambda i, index: (0, 0))
    return pl.pallas_call(
        total_kernel,
        out_shape=(
            jax.ShapeDtypeStruct((blocks * side, width), jnp.float32),
            jax.ShapeDtypeStruct((width, width), jnp.float32),
        ),
        grid_spec=pltpu.PrefetchScalarGridSpec(
            num_scalar_prefetch=1,
            grid=(1,),
            in_specs=[
                pl.BlockSpec((1, blocks, side, width), lambda i, index: (index[0], 0, 0, 0)),
                pl.BlockSpec((1, length, width), lambda i, index: (index[0], 0, 0)),
                whole,
                whole,
                whole,
            ],
            out_specs=(
                pl.BlockSpec((blocks * side, width), lambda i, index: (0, 0)),
                pl.BlockSpec((width, width), lambda i, index: (0, 0)),
            ),
        ),
        compiler_params=pltpu.CompilerParams(vmem_limit_bytes=VMEM),
        name="total_sum",
    )(index, keep, received, *others)


def swap(value, axes, mask, size):
    return lax.ppermute(value, axes, [(i, i ^ mask) for i in range(size)])


def sum_four(value, axes, low, high, size):
    others = [swap(value, axes, m, size) for m in (low, high, low ^ high)]
    return (value + others[0]) + (others[1] + others[2])


def shards(tiles, tile_row, tile_owner, tile_offset, counts, sketch):
    row_count = lax.axis_size("row")
    col_count = lax.axis_size("col")
    slot_count, side = tiles.shape[1:3]
    width = sketch.shape[1]
    blocks = sketch.shape[0] // side
    place = lax.axis_index("col")
    core, chip = place % 2, place // 2
    live = counts[0]
    omega, table, early = gather_rows(sketch, side)
    tile_row, tile_owner, tile_offset, _ = lax.optimization_barrier((tile_row, tile_owner, tile_offset, early))
    rows = jnp.where(jnp.arange(slot_count, dtype=jnp.int32) < live, tile_row[0], col_count * blocks)
    order, starts, where, groups = plan(tile_owner[0, :, 0], tile_offset[0], live, table, len(omega), blocks)
    meta = jnp.stack([groups, core]).astype(jnp.int32)
    keep, send = products(tiles[0], omega, order, starts, where, rows, meta, col_count // 2, blocks)

    received = swap(send, "col", 1, col_count)
    others = []
    for k in (2, 1, 3):
        coded = half_sum((chip ^ k).reshape(1), keep, received)
        others.append(swap(coded, "col", 2 * k, col_count))
    sampled, local_gram = total_sum(chip.reshape(1), keep, received, others)

    both = ("row", "col")
    devices = row_count * col_count
    gram = sum_four(local_gram, both, 1, 4 * col_count, devices)
    gram = sum_four(gram, both, 2, 4, devices)
    gram = sum_four(gram, both, col_count, 2 * col_count, devices)
    gram = sum_four(gram, both, 8 * col_count, 16 * col_count, devices)
    gram = gram / (sampled.shape[0] * devices)
    lower = jnp.linalg.cholesky(gram)
    solved = jax.scipy.linalg.solve_triangular(lower, sampled.T, lower=True)
    return (solved.T, lower.T)


def solution(mesh):
    in_specs = (
        P(("row", "col"), None, None, None),
        P(("row", "col"), None),
        P(("row", "col"), None, None),
        P(("row", "col"), None),
        P(("row", "col")),
        P(("col", "row"), None),
    )
    out_specs = (P(("row", "col"), None), P())
    return jax.shard_map(shards, mesh=mesh, in_specs=in_specs, out_specs=out_specs, check_vma=False)
```

```python
import jax
import jax.numpy as jnp
import numpy as np
from jax import lax
from jax.experimental import pallas as pl
from jax.experimental.pallas import tpu as pltpu
from jax.sharding import PartitionSpec as P

GROUP = 8
VMEM = 60 * 1024 * 1024
SMALL_VMEM = 40 * 1024 * 1024
PANEL = 32
Y_SIZE = 4
Z_SIZE = 8
FIRST_SHARE = 10
HIGHEST = lax.Precision.HIGHEST


def encode(value):
    top = jnp.max(jnp.abs(value), axis=0, keepdims=True)
    top = jnp.maximum(top, 1e-28) * 1.0001
    power = jnp.floor(jnp.log2(top)) - 14.0
    scaled = jnp.round(value * jnp.exp2(-power))
    coded = jnp.clip(scaled, -32767.0, 32767.0).astype(jnp.int32).astype(jnp.int16)
    return coded, power


def encode_block(get_tile, coded_ref, side, count):
    powers = jnp.zeros((count, side), jnp.float32)
    which = lax.broadcasted_iota(jnp.int32, (count, side), 0)

    def one(t, powers):
        coded, power = encode(get_tile(t))
        coded_ref[pl.ds(pl.multiple_of(t * side, side), side), :] = coded
        return jnp.where(which == t, power, powers)

    powers = lax.fori_loop(0, count, one, powers, unroll=2)
    coded_ref[pl.ds(count * side, count), :] = powers.astype(jnp.int32).astype(jnp.int16)


def decode_scales(coded_ref, side, count):
    return jnp.exp2(coded_ref[pl.ds(count * side, count), :].astype(jnp.int32).astype(jnp.float32))


class Piece:
    def __init__(self, array, runs):
        self.array = array
        self.runs = runs

    @property
    def blocks(self):
        return sum(run[3] for run in self.runs)


def cut(piece, first, count, side):
    runs, at = [], 0
    for y, z, start, blocks in piece.runs:
        low, high = max(first, at), min(first + count, at + blocks)
        if high > low:
            runs.append((y, z, start + low - at, high - low))
        at += blocks
    return Piece(piece.array[first * side : (first + count) * side], runs)


def join(pieces):
    return Piece(jnp.concatenate([p.array for p in pieces], 0), [r for p in pieces for r in p.runs])


def shift(piece, dy, dz, after=()):
    array = piece.array
    if after:
        array = lax.optimization_barrier((array,) + tuple(p.array for p in after))[0]
    pairs = [
        (y * Z_SIZE + z, (y + dy) % Y_SIZE * Z_SIZE + (z + dz) % Z_SIZE)
        for y in range(Y_SIZE)
        for z in range(Z_SIZE)
    ]
    runs = [((y - dy) % Y_SIZE, (z - dz) % Z_SIZE, start, n) for y, z, start, n in piece.runs]
    return Piece(lax.ppermute(array, "row", pairs), runs)


def gather_rows(sketch, side):
    def both_y(up, down, after=()):
        return shift(up, 1, 0, after), shift(down, -1, 0, after)

    def both_z(up, down, after=()):
        return shift(up, 0, 1, after), shift(down, 0, -1, after)

    def halves(pair):
        half = pair[0].blocks // 2
        return cut(pair[0], 0, half, side), cut(pair[1], half, pair[1].blocks - half, side)

    blocks = sketch.shape[0] // side
    a = Piece(sketch[: FIRST_SHARE * side], [(0, 0, 0, FIRST_SHARE)])
    b = Piece(sketch[FIRST_SHARE * side :], [(0, 0, FIRST_SHARE, blocks - FIRST_SHARE)])
    za1 = both_z(a, a)
    yb = both_y(b, b)
    ya = both_y(a, a)
    za2 = both_z(*za1)
    yb2 = both_y(*halves(yb))
    za3 = both_z(*za2, after=yb)
    ya2 = both_y(*halves(ya), after=yb)
    p1 = join(za1)
    y1 = both_y(p1, p1, after=yb2)
    z4 = both_z(*halves(za3), after=ya2)
    around = join([b, *yb, *yb2])
    zb1 = both_z(around, around, after=za2)
    p2 = join(za2)
    y2 = both_y(p2, p2, after=ya2)
    zb2 = both_z(*zb1, after=y1 + z4)
    p3 = join([*za3, *z4])
    y3 = both_y(p3, p3, after=y1)
    h1, h2 = halves(y1), halves(y2)
    f1 = both_y(join([h1[0], h2[0]]), join([h1[1], h2[1]]), after=zb1)
    zb3 = both_z(*zb2, after=y3)
    f2 = both_y(*halves(y3))
    zb4 = both_z(*halves(zb3), after=f1)
    pieces = [a, *ya, *ya2, p1, *y1, p2, *y2, p3, *y3, *f1, *f2, around, *zb1, *zb2, *zb3, *zb4]
    table = np.full((Y_SIZE * Z_SIZE * blocks, 2), -1, np.int32)
    for number, piece in enumerate(pieces):
        at = 0
        for y, z, start, count in piece.runs:
            for i in range(count):
                table[(y * Z_SIZE + z) * blocks + start + i] = (number, at)
                at += 1
    assert (table >= 0).all() and sum(p.blocks for p in pieces) == len(table)
    arrays = [p.array.reshape(p.blocks, side, sketch.shape[1]) for p in pieces]
    return arrays, table, yb[0].array


def products_kernel(count, order, starts, place, rows, meta, tiles, *refs):
    omega, (keep, send, tile_buf, omega_buf, total, coded) = refs[:count], refs[count : count + 6]
    tile_sem, omega_sem, keep_sem, send_sem = refs[count + 6 :]
    groups = meta[0]
    core = meta[1]
    side = tiles.shape[1]
    halves = keep.shape[0]
    blocks = (total.shape[0] - 1) // (2 * halves)

    def tile_copy(group):
        part = pl.ds(group * GROUP, GROUP)
        return pltpu.make_async_copy(tiles.at[part], tile_buf.at[part], tile_sem.at[group])

    def fetch_tiles(group, _):
        tile_copy(group).start()
        return 0

    lax.fori_loop(0, groups, fetch_tiles, 0)
    for p in range(count):

        def fetch(j, _, p=p):
            slot = order[j]
            pltpu.make_async_copy(
                omega[p].at[place[slot]], omega_buf.at[slot], omega_sem.at[slot // GROUP]
            ).start()
            return 0

        lax.fori_loop(starts[p], starts[p + 1], fetch, 0)

    def clear(t, _):
        total[t] = jnp.zeros(total.shape[1:], jnp.float32)
        return 0

    lax.fori_loop(0, total.shape[0], clear, 0)

    def step(group, _):
        first = group * GROUP
        tile_copy(group).wait()
        pltpu.make_async_copy(
            tiles.at[pl.ds(0, GROUP)], omega_buf.at[pl.ds(first, GROUP)], omega_sem.at[group]
        ).wait()
        parts = [
            jnp.dot(tile_buf[first + i], omega_buf[first + i], preferred_element_type=jnp.float32)
            for i in range(GROUP)
        ]
        for i in range(GROUP):
            total[rows[first + i]] += parts[i]
        return 0

    lax.fori_loop(0, groups, step, 0)

    def keep_copy(x):
        return pltpu.make_async_copy(
            total.at[pl.ds((2 * x + core) * blocks, blocks)], keep.at[x], keep_sem.at[x]
        )

    def send_copy(x):
        return pltpu.make_async_copy(coded.at[x], send.at[x], send_sem.at[x])

    for x in range(halves):
        keep_copy(x).start()
    for x in range(halves):
        first = (2 * x + 1 - core) * blocks
        encode_block(lambda t: total[first + t], coded.at[x], side, blocks)
        send_copy(x).start()
    for x in range(halves):
        keep_copy(x).wait()
        send_copy(x).wait()


def products(tiles, omega, order, starts, place, rows, meta, halves, blocks):
    slots, side, _ = tiles.shape
    width = omega[0].shape[2]
    panel = 2 * halves * blocks
    any_spec = pl.BlockSpec(memory_space=pl.ANY)
    return pl.pallas_call(
        lambda *refs: products_kernel(len(omega), *refs),
        out_shape=(
            jax.ShapeDtypeStruct((halves, blocks, side, width), jnp.float32),
            jax.ShapeDtypeStruct((halves, blocks * side + blocks, width), jnp.int16),
        ),
        grid_spec=pltpu.PrefetchScalarGridSpec(
            num_scalar_prefetch=5,
            grid=(1,),
            in_specs=[any_spec] * (1 + len(omega)),
            out_specs=(any_spec, any_spec),
            scratch_shapes=[
                pltpu.VMEM((slots, side, side), jnp.bfloat16),
                pltpu.VMEM((slots, side, width), jnp.bfloat16),
                pltpu.VMEM((panel + 1, side, width), jnp.float32),
                pltpu.VMEM((halves, blocks * side + blocks, width), jnp.int16),
                pltpu.SemaphoreType.DMA((slots // GROUP,)),
                pltpu.SemaphoreType.DMA((slots // GROUP,)),
                pltpu.SemaphoreType.DMA((halves,)),
                pltpu.SemaphoreType.DMA((halves,)),
            ],
        ),
        compiler_params=pltpu.CompilerParams(vmem_limit_bytes=VMEM),
        cost_estimate=pl.CostEstimate(flops=2 * slots * side**3, bytes_accessed=24 << 20, transcendentals=0),
        name="products",
    )(order, starts, place, rows, meta, tiles, *omega)


def plan(owner, offset, live, table, pieces, blocks):
    slots = owner.shape[0]
    here = lax.axis_index("row")
    y = (owner // Z_SIZE - here // Z_SIZE) % Y_SIZE
    z = (owner % Z_SIZE - here % Z_SIZE) % Z_SIZE
    code = (y * Z_SIZE + z) * blocks + offset
    chosen = code[:, None] == jnp.arange(len(table), dtype=jnp.int32)[None, :]
    piece = jnp.sum(jnp.where(chosen, jnp.asarray(table[:, 0])[None, :], 0), 1)
    place = jnp.sum(jnp.where(chosen, jnp.asarray(table[:, 1])[None, :], 0), 1)
    groups = (live + GROUP - 1) // GROUP
    number = jnp.arange(slots, dtype=jnp.int32)
    key = jnp.where(number < groups * GROUP, piece, pieces)
    key = key * slots + number
    rank = jnp.sum((key[None, :] < key[:, None]).astype(jnp.int32), 1)
    order = jnp.sum(jnp.where(rank[None, :] == number[:, None], number[None, :], 0), 1)
    limits = jnp.arange(pieces + 1, dtype=jnp.int32) * slots
    starts = jnp.sum((key[None, :] < limits[:, None]).astype(jnp.int32), 1)
    return order, starts, place, groups


def half_sum_kernel(index, keep, received, coded):
    blocks, side = keep.shape[1:3]
    scales = decode_scales(received.at[0], side, blocks)
    which = lax.broadcasted_iota(jnp.int32, scales.shape, 0)

    def tile(t):
        scale = jnp.sum(jnp.where(which == t, scales, 0.0), axis=0, keepdims=True)
        rows = received[0, pl.ds(pl.multiple_of(t * side, side), side), :]
        return keep[0, t] + rows.astype(jnp.int32).astype(jnp.float32) * scale

    encode_block(tile, coded, side, blocks)


def half_sum(index, keep, received):
    _, blocks, side, width = keep.shape
    length = received.shape[1]
    return pl.pallas_call(
        half_sum_kernel,
        out_shape=jax.ShapeDtypeStruct((length, width), jnp.int16),
        grid_spec=pltpu.PrefetchScalarGridSpec(
            num_scalar_prefetch=1,
            grid=(1,),
            in_specs=[
                pl.BlockSpec((1, blocks, side, width), lambda i, index: (index[0], 0, 0, 0)),
                pl.BlockSpec((1, length, width), lambda i, index: (index[0], 0, 0)),
            ],
            out_specs=pl.BlockSpec((length, width), lambda i, index: (0, 0)),
        ),
        compiler_params=pltpu.CompilerParams(vmem_limit_bytes=SMALL_VMEM),
        cost_estimate=pl.CostEstimate(flops=1 << 22, bytes_accessed=2 << 20, transcendentals=0),
        name="half_sum",
    )(index, keep, received)


def total_kernel(index, keep, received, first, second, third, sampled, gram):
    blocks, side = keep.shape[1:3]
    parts = [received.at[0], first, second, third]
    scales = [decode_scales(p, side, blocks) for p in parts]
    which = lax.broadcasted_iota(jnp.int32, scales[0].shape, 0)

    def tile(t, _):
        rows = pl.ds(pl.multiple_of(t * side, side), side)
        terms = [keep[0, t]]
        for p, s in zip(parts, scales):
            scale = jnp.sum(jnp.where(which == t, s, 0.0), axis=0, keepdims=True)
            terms.append(p[rows, :].astype(jnp.int32).astype(jnp.float32) * scale)
        sampled[rows, :] = (terms[0] + terms[1]) + (terms[2] + terms[3]) + terms[4]
        return 0

    lax.fori_loop(0, blocks, tile, 0)
    piece = 4 * side
    acc = None
    for i in range(blocks // 4):
        part = sampled[pl.ds(i * piece, piece), :]
        term = lax.dot_general(
            part, part, (((0,), (0,)), ((), ())), precision=HIGHEST, preferred_element_type=jnp.float32
        )
        acc = term if acc is None else acc + term
    gram[...] = acc


def total_sum(index, keep, received, others):
    _, blocks, side, width = keep.shape
    length = received.shape[1]
    whole = pl.BlockSpec((length, width), lambda i, index: (0, 0))
    return pl.pallas_call(
        total_kernel,
        out_shape=(
            jax.ShapeDtypeStruct((blocks * side, width), jnp.float32),
            jax.ShapeDtypeStruct((width, width), jnp.float32),
        ),
        grid_spec=pltpu.PrefetchScalarGridSpec(
            num_scalar_prefetch=1,
            grid=(1,),
            in_specs=[
                pl.BlockSpec((1, blocks, side, width), lambda i, index: (index[0], 0, 0, 0)),
                pl.BlockSpec((1, length, width), lambda i, index: (index[0], 0, 0)),
                whole,
                whole,
                whole,
            ],
            out_specs=(
                pl.BlockSpec((blocks * side, width), lambda i, index: (0, 0)),
                pl.BlockSpec((width, width), lambda i, index: (0, 0)),
            ),
        ),
        compiler_params=pltpu.CompilerParams(vmem_limit_bytes=SMALL_VMEM),
        name="total_sum",
    )(index, keep, received, *others)


def finish_kernel(order, gram, sampled, basis, factor, work):
    n = gram.shape[0]
    row = lax.broadcasted_iota(jnp.int32, (n, n), 0)
    column = lax.broadcasted_iota(jnp.int32, (n, n), 1)
    work[:, :n] = gram[...] * (1.0 / order)
    work[:, n:] = jnp.where(row == column, 1.0, 0.0)
    inside = lax.broadcasted_iota(jnp.int32, (PANEL, 1), 0)
    for base in range(0, n, PANEL):
        end = base + PANEL
        part = work[base:end, :]
        pivots = jnp.zeros((PANEL, 1), jnp.float32)
        for j in range(PANEL):
            pivot_row = part[j : j + 1, :]
            pivot = pivot_row[:, base + j : base + j + 1]
            pivots = jnp.where(inside == j, pivot, pivots)
            if j + 1 < PANEL:
                below = jnp.where(inside > j, part[:, base + j : base + j + 1] * (1.0 / pivot), 0.0)
                part = part - below * pivot_row
        part = part * (1.0 / jnp.sqrt(pivots))
        work[base:end, :] = part
        if end < n:
            work[end:, :] -= lax.dot_general(
                part[:, end:n],
                part,
                (((0,), (0,)), ((), ())),
                precision=HIGHEST,
                preferred_element_type=jnp.float32,
            )
    factor[...] = jnp.where(column >= row, work[:, :n], 0.0)
    inverse = work[:, n:]
    piece = 4 * n
    for i in range(sampled.shape[0] // piece):
        rows = pl.ds(i * piece, piece)
        basis[rows, :] = lax.dot_general(
            sampled[rows, :],
            inverse,
            (((1,), (1,)), ((), ())),
            precision=HIGHEST,
            preferred_element_type=jnp.float32,
        )


def finish(order, gram, sampled):
    n = gram.shape[0]
    return pl.pallas_call(
        lambda *refs: finish_kernel(order, *refs),
        out_shape=(
            jax.ShapeDtypeStruct(sampled.shape, jnp.float32),
            jax.ShapeDtypeStruct(gram.shape, jnp.float32),
        ),
        scratch_shapes=[pltpu.VMEM((n, 2 * n), jnp.float32)],
        compiler_params=pltpu.CompilerParams(vmem_limit_bytes=SMALL_VMEM),
        name="finish",
    )(gram, sampled)


def swap(value, axes, mask, size):
    return lax.ppermute(value, axes, [(i, i ^ mask) for i in range(size)])


def sum_four(value, axes, low, high, size):
    others = [swap(value, axes, m, size) for m in (low, high, low ^ high)]
    return (value + others[0]) + (others[1] + others[2])


def shards(tiles, tile_row, tile_owner, tile_offset, counts, sketch):
    row_count = lax.axis_size("row")
    col_count = lax.axis_size("col")
    slot_count, side = tiles.shape[1:3]
    width = sketch.shape[1]
    blocks = sketch.shape[0] // side
    place = lax.axis_index("col")
    core, chip = place % 2, place // 2
    live = counts[0]
    omega, table, early = gather_rows(sketch, side)
    tile_row, tile_owner, tile_offset, _ = lax.optimization_barrier((tile_row, tile_owner, tile_offset, early))
    rows = jnp.where(jnp.arange(slot_count, dtype=jnp.int32) < live, tile_row[0], col_count * blocks)
    order, starts, where, groups = plan(tile_owner[0, :, 0], tile_offset[0], live, table, len(omega), blocks)
    meta = jnp.stack([groups, core]).astype(jnp.int32)
    keep, send = products(tiles[0], omega, order, starts, where, rows, meta, col_count // 2, blocks)

    received = swap(send, "col", 1, col_count)
    others = []
    for k in (2, 1, 3):
        coded = half_sum((chip ^ k).reshape(1), keep, received)
        others.append(swap(coded, "col", 2 * k, col_count))
    sampled, local_gram = total_sum(chip.reshape(1), keep, received, others)

    both = ("row", "col")
    devices = row_count * col_count
    gram = sum_four(local_gram, both, 1, 4 * col_count, devices)
    gram = sum_four(gram, both, 2, 4, devices)
    gram = sum_four(gram, both, col_count, 2 * col_count, devices)
    gram = sum_four(gram, both, 8 * col_count, 16 * col_count, devices)
    return finish(sampled.shape[0] * devices, gram, sampled)


def solution(mesh):
    in_specs = (
        P(("row", "col"), None, None, None),
        P(("row", "col"), None),
        P(("row", "col"), None, None),
        P(("row", "col"), None),
        P(("row", "col")),
        P(("col", "row"), None),
    )
    out_specs = (P(("row", "col"), None), P())
    return jax.shard_map(shards, mesh=mesh, in_specs=in_specs, out_specs=out_specs, check_vma=False)
```

```python
import jax
import jax.numpy as jnp
import numpy as np
from jax import lax
from jax.experimental import pallas as pl
from jax.experimental.pallas import tpu as pltpu
from jax.sharding import PartitionSpec as P

GROUP = 8
VMEM = 28 * 1024 * 1024
SMALL_VMEM = 40 * 1024 * 1024
PANEL = 32
Y_SIZE = 4
Z_SIZE = 8
FIRST_SHARE = 10
HIGHEST = lax.Precision.HIGHEST


def encode(value):
    top = jnp.max(jnp.abs(value), axis=0, keepdims=True)
    top = jnp.maximum(top, 1e-28) * 1.0001
    power = jnp.floor(jnp.log2(top)) - 14.0
    scaled = jnp.round(value * jnp.exp2(-power))
    coded = jnp.clip(scaled, -32767.0, 32767.0).astype(jnp.int32).astype(jnp.int16)
    return coded, power


def encode_block(get_tile, coded_ref, side, count):
    powers = jnp.zeros((count, side), jnp.float32)
    which = lax.broadcasted_iota(jnp.int32, (count, side), 0)

    def one(t, powers):
        coded, power = encode(get_tile(t))
        coded_ref[pl.ds(pl.multiple_of(t * side, side), side), :] = coded
        return jnp.where(which == t, power, powers)

    powers = lax.fori_loop(0, count, one, powers, unroll=2)
    coded_ref[pl.ds(count * side, count), :] = powers.astype(jnp.int32).astype(jnp.int16)


def decode_scales(coded_ref, side, count):
    return jnp.exp2(coded_ref[pl.ds(count * side, count), :].astype(jnp.int32).astype(jnp.float32))


class Piece:
    def __init__(self, array, runs):
        self.array = array
        self.runs = runs

    @property
    def blocks(self):
        return sum(run[3] for run in self.runs)


def cut(piece, first, count, side):
    runs, at = [], 0
    for y, z, start, blocks in piece.runs:
        low, high = max(first, at), min(first + count, at + blocks)
        if high > low:
            runs.append((y, z, start + low - at, high - low))
        at += blocks
    return Piece(piece.array[first * side : (first + count) * side], runs)


def join(pieces):
    return Piece(jnp.concatenate([p.array for p in pieces], 0), [r for p in pieces for r in p.runs])


def shift(piece, dy, dz, after=()):
    array = piece.array
    if after:
        array = lax.optimization_barrier((array,) + tuple(p.array for p in after))[0]
    pairs = [
        (y * Z_SIZE + z, (y + dy) % Y_SIZE * Z_SIZE + (z + dz) % Z_SIZE)
        for y in range(Y_SIZE)
        for z in range(Z_SIZE)
    ]
    runs = [((y - dy) % Y_SIZE, (z - dz) % Z_SIZE, start, n) for y, z, start, n in piece.runs]
    return Piece(lax.ppermute(array, "row", pairs), runs)


def gather_rows(sketch, side):
    def both_y(up, down, after=()):
        return shift(up, 1, 0, after), shift(down, -1, 0, after)

    def both_z(up, down, after=()):
        return shift(up, 0, 1, after), shift(down, 0, -1, after)

    def halves(pair):
        half = pair[0].blocks // 2
        return cut(pair[0], 0, half, side), cut(pair[1], half, pair[1].blocks - half, side)

    blocks = sketch.shape[0] // side
    a = Piece(sketch[: FIRST_SHARE * side], [(0, 0, 0, FIRST_SHARE)])
    b = Piece(sketch[FIRST_SHARE * side :], [(0, 0, FIRST_SHARE, blocks - FIRST_SHARE)])
    za1 = both_z(a, a)
    yb = both_y(b, b)
    ya = both_y(a, a)
    za2 = both_z(*za1)
    yb2 = both_y(*halves(yb))
    za3 = both_z(*za2, after=yb)
    ya2 = both_y(*halves(ya), after=yb)
    p1 = join(za1)
    y1 = both_y(p1, p1, after=yb2)
    around = join([b, *yb, *yb2])
    zb1 = both_z(around, around, after=za2)
    z4 = both_z(*halves(za3), after=ya2)
    p2 = join(za2)
    y2 = both_y(p2, p2, after=ya2)
    zb2 = both_z(*zb1, after=y1 + z4)
    p3 = join(za3)
    y3 = both_y(p3, p3, after=y1)
    h1, h2 = halves(y1), halves(y2)
    f1 = both_y(join([h1[0], h2[0], *z4]), join([h1[1], h2[1], *z4]), after=zb1)
    zb3 = both_z(*zb2, after=y3)
    h3, last, first = halves(y3), z4[0].blocks + z4[1].blocks, h1[0].blocks + h2[0].blocks
    half = last // 2
    f2 = both_y(
        join([h3[0], cut(f1[0], first, half, side)]),
        join([h3[1], cut(f1[1], first + half, last - half, side)]),
    )
    zb4 = both_z(*halves(zb3), after=f1)
    pieces = [a, *ya, *ya2, p1, *y1, p2, *y2, p3, *y3, *z4, *f1, *f2, around, *zb1, *zb2, *zb3, *zb4]
    table = np.full((Y_SIZE * Z_SIZE * blocks, 2), -1, np.int32)
    for number, piece in enumerate(pieces):
        at = 0
        for y, z, start, count in piece.runs:
            for i in range(count):
                table[(y * Z_SIZE + z) * blocks + start + i] = (number, at)
                at += 1
    assert (table >= 0).all() and sum(p.blocks for p in pieces) == len(table)
    arrays = [p.array.reshape(p.blocks, side, sketch.shape[1]) for p in pieces]
    return arrays, table, yb[0].array


def products_kernel(count, order, starts, place, rows, meta, tiles, *refs):
    omega, (keep, send, tile_buf, omega_buf, total, coded) = refs[:count], refs[count : count + 6]
    tile_sem, omega_sem, keep_sem, send_sem = refs[count + 6 :]
    groups = meta[0]
    core = meta[1]
    side = tiles.shape[1]
    halves = keep.shape[0]
    blocks = (total.shape[0] - 1) // (2 * halves)

    def tile_copy(group):
        part = pl.ds(group * GROUP, GROUP)
        return pltpu.make_async_copy(tiles.at[part], tile_buf.at[part], tile_sem.at[group])

    def fetch_tiles(group, _):
        tile_copy(group).start()
        return 0

    lax.fori_loop(0, groups, fetch_tiles, 0)
    for p in range(count):

        def fetch(j, _, p=p):
            slot = order[j]
            pltpu.make_async_copy(
                omega[p].at[place[slot]], omega_buf.at[slot], omega_sem.at[slot // GROUP]
            ).start()
            return 0

        lax.fori_loop(starts[p], starts[p + 1], fetch, 0)

    def clear(t, _):
        total[t] = jnp.zeros(total.shape[1:], jnp.float32)
        return 0

    lax.fori_loop(0, total.shape[0], clear, 0)

    def step(group, _):
        first = group * GROUP
        tile_copy(group).wait()
        pltpu.make_async_copy(
            tiles.at[pl.ds(0, GROUP)], omega_buf.at[pl.ds(first, GROUP)], omega_sem.at[group]
        ).wait()
        parts = [
            jnp.dot(tile_buf[first + i], omega_buf[first + i], preferred_element_type=jnp.float32)
            for i in range(GROUP)
        ]
        for i in range(GROUP):
            total[rows[first + i]] += parts[i]
        return 0

    lax.fori_loop(0, groups, step, 0)

    def keep_copy(x):
        return pltpu.make_async_copy(
            total.at[pl.ds((2 * x + core) * blocks, blocks)], keep.at[x], keep_sem.at[x]
        )

    def send_copy(x):
        return pltpu.make_async_copy(coded.at[x], send.at[x], send_sem.at[x])

    for x in range(halves):
        keep_copy(x).start()
    for x in range(halves):
        first = (2 * x + 1 - core) * blocks
        encode_block(lambda t: total[first + t], coded.at[x], side, blocks)
        send_copy(x).start()
    for x in range(halves):
        keep_copy(x).wait()
        send_copy(x).wait()


def products(tiles, omega, order, starts, place, rows, meta, halves, blocks):
    slots, side, _ = tiles.shape
    width = omega[0].shape[2]
    panel = 2 * halves * blocks
    any_spec = pl.BlockSpec(memory_space=pl.ANY)
    return pl.pallas_call(
        lambda *refs: products_kernel(len(omega), *refs),
        out_shape=(
            pltpu.VMEM((halves, blocks, side, width), jnp.float32),
            pltpu.VMEM((halves, blocks * side + blocks, width), jnp.int16),
        ),
        grid_spec=pltpu.PrefetchScalarGridSpec(
            num_scalar_prefetch=5,
            grid=(1,),
            in_specs=[any_spec] * (1 + len(omega)),
            out_specs=(any_spec, any_spec),
            scratch_shapes=[
                pltpu.VMEM((slots, side, side), jnp.bfloat16),
                pltpu.VMEM((slots, side, width), jnp.bfloat16),
                pltpu.VMEM((panel + 1, side, width), jnp.float32),
                pltpu.VMEM((halves, blocks * side + blocks, width), jnp.int16),
                pltpu.SemaphoreType.DMA((slots // GROUP,)),
                pltpu.SemaphoreType.DMA((slots // GROUP,)),
                pltpu.SemaphoreType.DMA((halves,)),
                pltpu.SemaphoreType.DMA((halves,)),
            ],
        ),
        compiler_params=pltpu.CompilerParams(vmem_limit_bytes=VMEM),
        cost_estimate=pl.CostEstimate(flops=2 * slots * side**3, bytes_accessed=24 << 20, transcendentals=0),
        name="products",
    )(order, starts, place, rows, meta, tiles, *omega)


def plan(owner, offset, live, table, pieces, blocks):
    slots = owner.shape[0]
    here = lax.axis_index("row")
    y = (owner // Z_SIZE - here // Z_SIZE) % Y_SIZE
    z = (owner % Z_SIZE - here % Z_SIZE) % Z_SIZE
    code = (y * Z_SIZE + z) * blocks + offset
    chosen = code[:, None] == jnp.arange(len(table), dtype=jnp.int32)[None, :]
    piece = jnp.sum(jnp.where(chosen, jnp.asarray(table[:, 0])[None, :], 0), 1)
    place = jnp.sum(jnp.where(chosen, jnp.asarray(table[:, 1])[None, :], 0), 1)
    groups = (live + GROUP - 1) // GROUP
    number = jnp.arange(slots, dtype=jnp.int32)
    key = jnp.where(number < groups * GROUP, piece, pieces)
    key = key * slots + number
    rank = jnp.sum((key[None, :] < key[:, None]).astype(jnp.int32), 1)
    order = jnp.sum(jnp.where(rank[None, :] == number[:, None], number[None, :], 0), 1)
    limits = jnp.arange(pieces + 1, dtype=jnp.int32) * slots
    starts = jnp.sum((key[None, :] < limits[:, None]).astype(jnp.int32), 1)
    return order, starts, place, groups


def half_sum_kernel(index, keep, received, coded):
    blocks, side = keep.shape[1:3]
    scales = decode_scales(received.at[0], side, blocks)
    which = lax.broadcasted_iota(jnp.int32, scales.shape, 0)

    def tile(t):
        scale = jnp.sum(jnp.where(which == t, scales, 0.0), axis=0, keepdims=True)
        rows = received[0, pl.ds(pl.multiple_of(t * side, side), side), :]
        return keep[0, t] + rows.astype(jnp.int32).astype(jnp.float32) * scale

    encode_block(tile, coded, side, blocks)


def half_sum(index, keep, received):
    _, blocks, side, width = keep.shape
    length = received.shape[1]
    return pl.pallas_call(
        half_sum_kernel,
        out_shape=jax.ShapeDtypeStruct((length, width), jnp.int16),
        grid_spec=pltpu.PrefetchScalarGridSpec(
            num_scalar_prefetch=1,
            grid=(1,),
            in_specs=[
                pl.BlockSpec((1, blocks, side, width), lambda i, index: (index[0], 0, 0, 0)),
                pl.BlockSpec((1, length, width), lambda i, index: (index[0], 0, 0)),
            ],
            out_specs=pl.BlockSpec((length, width), lambda i, index: (0, 0)),
        ),
        compiler_params=pltpu.CompilerParams(vmem_limit_bytes=SMALL_VMEM),
        cost_estimate=pl.CostEstimate(flops=1 << 22, bytes_accessed=2 << 20, transcendentals=0),
        name="half_sum",
    )(index, keep, received)


def total_kernel(index, keep, received, first, second, third, sampled, gram):
    blocks, side = keep.shape[1:3]
    parts = [received.at[0], first, second, third]
    scales = [decode_scales(p, side, blocks) for p in parts]
    which = lax.broadcasted_iota(jnp.int32, scales[0].shape, 0)

    def tile(t, _):
        rows = pl.ds(pl.multiple_of(t * side, side), side)
        terms = [keep[0, t]]
        for p, s in zip(parts, scales):
            scale = jnp.sum(jnp.where(which == t, s, 0.0), axis=0, keepdims=True)
            terms.append(p[rows, :].astype(jnp.int32).astype(jnp.float32) * scale)
        sampled[rows, :] = (terms[0] + terms[1]) + (terms[2] + terms[3]) + terms[4]
        return 0

    lax.fori_loop(0, blocks, tile, 0)
    piece = 4 * side
    acc = None
    for i in range(blocks // 4):
        part = sampled[pl.ds(i * piece, piece), :]
        term = lax.dot_general(
            part, part, (((0,), (0,)), ((), ())), precision=HIGHEST, preferred_element_type=jnp.float32
        )
        acc = term if acc is None else acc + term
    gram[...] = acc


def total_sum(index, keep, received, others):
    _, blocks, side, width = keep.shape
    length = received.shape[1]
    whole = pl.BlockSpec((length, width), lambda i, index: (0, 0))
    return pl.pallas_call(
        total_kernel,
        out_shape=(
            jax.ShapeDtypeStruct((blocks * side, width), jnp.float32),
            jax.ShapeDtypeStruct((width, width), jnp.float32),
        ),
        grid_spec=pltpu.PrefetchScalarGridSpec(
            num_scalar_prefetch=1,
            grid=(1,),
            in_specs=[
                pl.BlockSpec((1, blocks, side, width), lambda i, index: (index[0], 0, 0, 0)),
                pl.BlockSpec((1, length, width), lambda i, index: (index[0], 0, 0)),
                whole,
                whole,
                whole,
            ],
            out_specs=(
                pl.BlockSpec((blocks * side, width), lambda i, index: (0, 0)),
                pl.BlockSpec((width, width), lambda i, index: (0, 0)),
            ),
        ),
        compiler_params=pltpu.CompilerParams(vmem_limit_bytes=SMALL_VMEM),
        name="total_sum",
    )(index, keep, received, *others)


def finish_kernel(order, gram, sampled, basis, factor, work):
    n = gram.shape[0]
    row = lax.broadcasted_iota(jnp.int32, (n, n), 0)
    column = lax.broadcasted_iota(jnp.int32, (n, n), 1)
    work[:, :n] = gram[...] * (1.0 / order)
    work[:, n:] = jnp.where(row == column, 1.0, 0.0)
    inside = lax.broadcasted_iota(jnp.int32, (PANEL, 1), 0)
    for base in range(0, n, PANEL):
        end = base + PANEL
        part = work[base:end, :]
        pivots = jnp.zeros((PANEL, 1), jnp.float32)
        for j in range(PANEL):
            pivot_row = part[j : j + 1, :]
            pivot = pivot_row[:, base + j : base + j + 1]
            pivots = jnp.where(inside == j, pivot, pivots)
            if j + 1 < PANEL:
                below = jnp.where(inside > j, part[:, base + j : base + j + 1] * (1.0 / pivot), 0.0)
                part = part - below * pivot_row
        part = part * (1.0 / jnp.sqrt(pivots))
        work[base:end, :] = part
        if end < n:
            work[end:, :] -= lax.dot_general(
                part[:, end:n],
                part,
                (((0,), (0,)), ((), ())),
                precision=HIGHEST,
                preferred_element_type=jnp.float32,
            )
    factor[...] = jnp.where(column >= row, work[:, :n], 0.0)
    inverse = work[:, n:]
    piece = 4 * n
    for i in range(sampled.shape[0] // piece):
        rows = pl.ds(i * piece, piece)
        basis[rows, :] = lax.dot_general(
            sampled[rows, :],
            inverse,
            (((1,), (1,)), ((), ())),
            precision=HIGHEST,
            preferred_element_type=jnp.float32,
        )


def finish(order, gram, sampled):
    n = gram.shape[0]
    return pl.pallas_call(
        lambda *refs: finish_kernel(order, *refs),
        out_shape=(
            jax.ShapeDtypeStruct(sampled.shape, jnp.float32),
            jax.ShapeDtypeStruct(gram.shape, jnp.float32),
        ),
        scratch_shapes=[pltpu.VMEM((n, 2 * n), jnp.float32)],
        compiler_params=pltpu.CompilerParams(vmem_limit_bytes=SMALL_VMEM),
        name="finish",
    )(gram, sampled)


def swap(value, axes, mask, size):
    return lax.ppermute(value, axes, [(i, i ^ mask) for i in range(size)])


def sum_four(value, axes, low, high, size):
    others = [swap(value, axes, m, size) for m in (low, high, low ^ high)]
    return (value + others[0]) + (others[1] + others[2])


def shards(tiles, tile_row, tile_owner, tile_offset, counts, sketch):
    row_count = lax.axis_size("row")
    col_count = lax.axis_size("col")
    slot_count, side = tiles.shape[1:3]
    width = sketch.shape[1]
    blocks = sketch.shape[0] // side
    place = lax.axis_index("col")
    core, chip = place % 2, place // 2
    live = counts[0]
    omega, table, early = gather_rows(sketch, side)
    tile_row, tile_owner, tile_offset, _ = lax.optimization_barrier((tile_row, tile_owner, tile_offset, early))
    rows = jnp.where(jnp.arange(slot_count, dtype=jnp.int32) < live, tile_row[0], col_count * blocks)
    order, starts, where, groups = plan(tile_owner[0, :, 0], tile_offset[0], live, table, len(omega), blocks)
    meta = jnp.stack([groups, core]).astype(jnp.int32)
    keep, send = products(tiles[0], omega, order, starts, where, rows, meta, col_count // 2, blocks)

    received = swap(send, "col", 1, col_count)
    others = []
    for k in (2, 1, 3):
        coded = half_sum((chip ^ k).reshape(1), keep, received)
        others.append(swap(coded, "col", 2 * k, col_count))
    sampled, local_gram = total_sum(chip.reshape(1), keep, received, others)

    both = ("row", "col")
    devices = row_count * col_count
    gram = sum_four(local_gram, both, 1, 4 * col_count, devices)
    gram = sum_four(gram, both, 2, 4, devices)
    gram = sum_four(gram, both, col_count, 2 * col_count, devices)
    gram = sum_four(gram, both, 8 * col_count, 16 * col_count, devices)
    return finish(sampled.shape[0] * devices, gram, sampled)


def solution(mesh):
    in_specs = (
        P(("row", "col"), None, None, None),
        P(("row", "col"), None),
        P(("row", "col"), None, None),
        P(("row", "col"), None),
        P(("row", "col")),
        P(("col", "row"), None),
    )
    out_specs = (P(("row", "col"), None), P())
    return jax.shard_map(shards, mesh=mesh, in_specs=in_specs, out_specs=out_specs, check_vma=False)
```

```python
import jax
import jax.numpy as jnp
import numpy as np
from jax import lax
from jax.experimental import pallas as pl
from jax.experimental.pallas import tpu as pltpu
from jax.sharding import PartitionSpec as P

GROUP = 8
VMEM = 60 * 1024 * 1024
SMALL_VMEM = 40 * 1024 * 1024
PANEL = 32
Y_SIZE = 4
Z_SIZE = 8
FIRST_SHARE = 10
HIGHEST = lax.Precision.HIGHEST


def encode(value):
    top = jnp.max(jnp.abs(value), axis=0, keepdims=True)
    top = jnp.maximum(top, 1e-28) * 1.0001
    power = jnp.floor(jnp.log2(top)) - 14.0
    scaled = jnp.round(value * jnp.exp2(-power))
    coded = jnp.clip(scaled, -32767.0, 32767.0).astype(jnp.int32).astype(jnp.int16)
    return coded, power


def encode_block(get_tile, coded_ref, side, count):
    powers = jnp.zeros((count, side), jnp.float32)
    which = lax.broadcasted_iota(jnp.int32, (count, side), 0)

    def one(t, powers):
        coded, power = encode(get_tile(t))
        coded_ref[pl.ds(pl.multiple_of(t * side, side), side), :] = coded
        return jnp.where(which == t, power, powers)

    powers = lax.fori_loop(0, count, one, powers, unroll=2)
    coded_ref[pl.ds(count * side, count), :] = powers.astype(jnp.int32).astype(jnp.int16)


def decode_scales(coded_ref, side, count):
    return jnp.exp2(coded_ref[pl.ds(count * side, count), :].astype(jnp.int32).astype(jnp.float32))


class Piece:
    def __init__(self, array, runs):
        self.array = array
        self.runs = runs

    @property
    def blocks(self):
        return sum(run[3] for run in self.runs)


def cut(piece, first, count, side):
    runs, at = [], 0
    for y, z, start, blocks in piece.runs:
        low, high = max(first, at), min(first + count, at + blocks)
        if high > low:
            runs.append((y, z, start + low - at, high - low))
        at += blocks
    return Piece(piece.array[first * side : (first + count) * side], runs)


def join(pieces):
    return Piece(jnp.concatenate([p.array for p in pieces], 0), [r for p in pieces for r in p.runs])


def shift(piece, dy, dz, after=()):
    array = piece.array
    if after:
        array = lax.optimization_barrier((array,) + tuple(p.array for p in after))[0]
    pairs = [
        (y * Z_SIZE + z, (y + dy) % Y_SIZE * Z_SIZE + (z + dz) % Z_SIZE)
        for y in range(Y_SIZE)
        for z in range(Z_SIZE)
    ]
    runs = [((y - dy) % Y_SIZE, (z - dz) % Z_SIZE, start, n) for y, z, start, n in piece.runs]
    return Piece(lax.ppermute(array, "row", pairs), runs)


def gather_rows(sketch, side):
    def both_y(up, down, after=()):
        return shift(up, 1, 0, after), shift(down, -1, 0, after)

    def both_z(up, down, after=()):
        return shift(up, 0, 1, after), shift(down, 0, -1, after)

    def halves(pair):
        half = pair[0].blocks // 2
        return cut(pair[0], 0, half, side), cut(pair[1], half, pair[1].blocks - half, side)

    blocks = sketch.shape[0] // side
    a = Piece(sketch[: FIRST_SHARE * side], [(0, 0, 0, FIRST_SHARE)])
    b = Piece(sketch[FIRST_SHARE * side :], [(0, 0, FIRST_SHARE, blocks - FIRST_SHARE)])
    za1 = both_z(a, a)
    yb = both_y(b, b)
    ya = both_y(a, a)
    za2 = both_z(*za1)
    yb2 = both_y(*halves(yb))
    za3 = both_z(*za2, after=yb)
    ya2 = both_y(*halves(ya), after=yb)
    p1 = join(za1)
    y1 = both_y(p1, p1, after=ya2)
    around = join([b, *yb, *yb2])
    zb1 = both_z(around, around, after=za2)
    z4 = both_z(*halves(za3), after=ya2)
    p2 = join(za2)
    y2 = both_y(p2, p2, after=za3)
    zb2 = both_z(*zb1, after=y1 + z4)
    p3 = join(za3)
    y3 = both_y(p3, p3, after=y1)
    h1, h2 = halves(y1), halves(y2)
    f1 = both_y(join([h1[0], h2[0], *z4]), join([h1[1], h2[1], *z4]), after=zb1)
    zb3 = both_z(*zb2, after=y3)
    h3, last, first = halves(y3), z4[0].blocks + z4[1].blocks, h1[0].blocks + h2[0].blocks
    half = last // 2
    f2 = both_y(
        join([h3[0], cut(f1[0], first, half, side)]),
        join([h3[1], cut(f1[1], first + half, last - half, side)]),
    )
    zb4 = both_z(*halves(zb3), after=f1)
    pieces = [a, *ya, *ya2, p1, *y1, p2, *y2, p3, *y3, *z4, *f1, *f2, around, *zb1, *zb2, *zb3, *zb4]
    table = np.full((Y_SIZE * Z_SIZE * blocks, 2), -1, np.int32)
    for number, piece in enumerate(pieces):
        at = 0
        for y, z, start, count in piece.runs:
            for i in range(count):
                table[(y * Z_SIZE + z) * blocks + start + i] = (number, at)
                at += 1
    assert (table >= 0).all() and sum(p.blocks for p in pieces) == len(table)
    arrays = [p.array.reshape(p.blocks, side, sketch.shape[1]) for p in pieces]
    return arrays, table, yb[0].array


def products_kernel(count, order, starts, place, rows, meta, tiles, *refs):
    omega, (keep, send, tile_buf, omega_buf, total, coded) = refs[:count], refs[count : count + 6]
    tile_sem, omega_sem, keep_sem, send_sem = refs[count + 6 :]
    groups = meta[0]
    core = meta[1]
    side = tiles.shape[1]
    halves = keep.shape[0]
    blocks = (total.shape[0] - 1) // (2 * halves)

    def tile_copy(group):
        part = pl.ds(group * GROUP, GROUP)
        return pltpu.make_async_copy(tiles.at[part], tile_buf.at[part], tile_sem.at[group])

    def fetch_tiles(group, _):
        tile_copy(group).start()
        return 0

    lax.fori_loop(0, groups, fetch_tiles, 0)
    for p in range(count):

        def fetch(j, _, p=p):
            slot = order[j]
            pltpu.make_async_copy(
                omega[p].at[place[slot]], omega_buf.at[slot], omega_sem.at[slot // GROUP]
            ).start()
            return 0

        lax.fori_loop(starts[p], starts[p + 1], fetch, 0)

    def clear(t, _):
        total[t] = jnp.zeros(total.shape[1:], jnp.float32)
        return 0

    lax.fori_loop(0, total.shape[0], clear, 0)

    def step(group, _):
        first = group * GROUP
        tile_copy(group).wait()
        pltpu.make_async_copy(
            tiles.at[pl.ds(0, GROUP)], omega_buf.at[pl.ds(first, GROUP)], omega_sem.at[group]
        ).wait()
        parts = [
            jnp.dot(tile_buf[first + i], omega_buf[first + i], preferred_element_type=jnp.float32)
            for i in range(GROUP)
        ]
        for i in range(GROUP):
            total[rows[first + i]] += parts[i]
        return 0

    lax.fori_loop(0, groups, step, 0)

    def keep_copy(x):
        return pltpu.make_async_copy(
            total.at[pl.ds((2 * x + core) * blocks, blocks)], keep.at[x], keep_sem.at[x]
        )

    def send_copy(x):
        return pltpu.make_async_copy(coded.at[x], send.at[x], send_sem.at[x])

    for x in range(halves):
        keep_copy(x).start()
    for x in range(halves):
        first = (2 * x + 1 - core) * blocks
        encode_block(lambda t: total[first + t], coded.at[x], side, blocks)
        send_copy(x).start()
    for x in range(halves):
        keep_copy(x).wait()
        send_copy(x).wait()


def products(tiles, omega, order, starts, place, rows, meta, halves, blocks):
    slots, side, _ = tiles.shape
    width = omega[0].shape[2]
    panel = 2 * halves * blocks
    any_spec = pl.BlockSpec(memory_space=pl.ANY)
    return pl.pallas_call(
        lambda *refs: products_kernel(len(omega), *refs),
        out_shape=(
            jax.ShapeDtypeStruct((halves, blocks, side, width), jnp.float32),
            jax.ShapeDtypeStruct((halves, blocks * side + blocks, width), jnp.int16),
        ),
        grid_spec=pltpu.PrefetchScalarGridSpec(
            num_scalar_prefetch=5,
            grid=(1,),
            in_specs=[any_spec] * (1 + len(omega)),
            out_specs=(any_spec, any_spec),
            scratch_shapes=[
                pltpu.VMEM((slots, side, side), jnp.bfloat16),
                pltpu.VMEM((slots, side, width), jnp.bfloat16),
                pltpu.VMEM((panel + 1, side, width), jnp.float32),
                pltpu.VMEM((halves, blocks * side + blocks, width), jnp.int16),
                pltpu.SemaphoreType.DMA((slots // GROUP,)),
                pltpu.SemaphoreType.DMA((slots // GROUP,)),
                pltpu.SemaphoreType.DMA((halves,)),
                pltpu.SemaphoreType.DMA((halves,)),
            ],
        ),
        compiler_params=pltpu.CompilerParams(vmem_limit_bytes=VMEM),
        cost_estimate=pl.CostEstimate(flops=2 * slots * side**3, bytes_accessed=24 << 20, transcendentals=0),
        name="products",
    )(order, starts, place, rows, meta, tiles, *omega)


def plan(owner, offset, live, table, pieces, blocks):
    slots = owner.shape[0]
    here = lax.axis_index("row")
    y = (owner // Z_SIZE - here // Z_SIZE) % Y_SIZE
    z = (owner % Z_SIZE - here % Z_SIZE) % Z_SIZE
    code = (y * Z_SIZE + z) * blocks + offset
    chosen = code[:, None] == jnp.arange(len(table), dtype=jnp.int32)[None, :]
    piece = jnp.sum(jnp.where(chosen, jnp.asarray(table[:, 0])[None, :], 0), 1)
    place = jnp.sum(jnp.where(chosen, jnp.asarray(table[:, 1])[None, :], 0), 1)
    groups = (live + GROUP - 1) // GROUP
    number = jnp.arange(slots, dtype=jnp.int32)
    key = jnp.where(number < groups * GROUP, piece, pieces)
    key = key * slots + number
    rank = jnp.sum((key[None, :] < key[:, None]).astype(jnp.int32), 1)
    order = jnp.sum(jnp.where(rank[None, :] == number[:, None], number[None, :], 0), 1)
    limits = jnp.arange(pieces + 1, dtype=jnp.int32) * slots
    starts = jnp.sum((key[None, :] < limits[:, None]).astype(jnp.int32), 1)
    return order, starts, place, groups


def half_sum_kernel(index, keep, received, coded):
    blocks, side = keep.shape[1:3]
    scales = decode_scales(received.at[0], side, blocks)
    which = lax.broadcasted_iota(jnp.int32, scales.shape, 0)

    def tile(t):
        scale = jnp.sum(jnp.where(which == t, scales, 0.0), axis=0, keepdims=True)
        rows = received[0, pl.ds(pl.multiple_of(t * side, side), side), :]
        return keep[0, t] + rows.astype(jnp.int32).astype(jnp.float32) * scale

    encode_block(tile, coded, side, blocks)


def half_sum(index, keep, received):
    _, blocks, side, width = keep.shape
    length = received.shape[1]
    return pl.pallas_call(
        half_sum_kernel,
        out_shape=jax.ShapeDtypeStruct((length, width), jnp.int16),
        grid_spec=pltpu.PrefetchScalarGridSpec(
            num_scalar_prefetch=1,
            grid=(1,),
            in_specs=[
                pl.BlockSpec((1, blocks, side, width), lambda i, index: (index[0], 0, 0, 0)),
                pl.BlockSpec((1, length, width), lambda i, index: (index[0], 0, 0)),
            ],
            out_specs=pl.BlockSpec((length, width), lambda i, index: (0, 0)),
        ),
        compiler_params=pltpu.CompilerParams(vmem_limit_bytes=SMALL_VMEM),
        cost_estimate=pl.CostEstimate(flops=1 << 22, bytes_accessed=2 << 20, transcendentals=0),
        name="half_sum",
    )(index, keep, received)


def total_kernel(index, keep, received, first, second, third, sampled, gram):
    blocks, side = keep.shape[1:3]
    parts = [received.at[0], first, second, third]
    scales = [decode_scales(p, side, blocks) for p in parts]
    which = lax.broadcasted_iota(jnp.int32, scales[0].shape, 0)

    def tile(t, _):
        rows = pl.ds(pl.multiple_of(t * side, side), side)
        terms = [keep[0, t]]
        for p, s in zip(parts, scales):
            scale = jnp.sum(jnp.where(which == t, s, 0.0), axis=0, keepdims=True)
            terms.append(p[rows, :].astype(jnp.int32).astype(jnp.float32) * scale)
        sampled[rows, :] = (terms[0] + terms[1]) + (terms[2] + terms[3]) + terms[4]
        return 0

    lax.fori_loop(0, blocks, tile, 0)
    piece = 4 * side
    acc = None
    for i in range(blocks // 4):
        part = sampled[pl.ds(i * piece, piece), :]
        term = lax.dot_general(
            part, part, (((0,), (0,)), ((), ())), precision=HIGHEST, preferred_element_type=jnp.float32
        )
        acc = term if acc is None else acc + term
    gram[...] = acc


def total_sum(index, keep, received, others):
    _, blocks, side, width = keep.shape
    length = received.shape[1]
    whole = pl.BlockSpec((length, width), lambda i, index: (0, 0))
    return pl.pallas_call(
        total_kernel,
        out_shape=(
            jax.ShapeDtypeStruct((blocks * side, width), jnp.float32),
            jax.ShapeDtypeStruct((width, width), jnp.float32),
        ),
        grid_spec=pltpu.PrefetchScalarGridSpec(
            num_scalar_prefetch=1,
            grid=(1,),
            in_specs=[
                pl.BlockSpec((1, blocks, side, width), lambda i, index: (index[0], 0, 0, 0)),
                pl.BlockSpec((1, length, width), lambda i, index: (index[0], 0, 0)),
                whole,
                whole,
                whole,
            ],
            out_specs=(
                pl.BlockSpec((blocks * side, width), lambda i, index: (0, 0)),
                pl.BlockSpec((width, width), lambda i, index: (0, 0)),
            ),
        ),
        compiler_params=pltpu.CompilerParams(vmem_limit_bytes=SMALL_VMEM),
        name="total_sum",
    )(index, keep, received, *others)


def finish_kernel(order, gram, sampled, basis, factor, work):
    n = gram.shape[0]
    row = lax.broadcasted_iota(jnp.int32, (n, n), 0)
    column = lax.broadcasted_iota(jnp.int32, (n, n), 1)
    work[:, :n] = gram[...] * (1.0 / order)
    work[:, n:] = jnp.where(row == column, 1.0, 0.0)
    inside = lax.broadcasted_iota(jnp.int32, (PANEL, 1), 0)
    for base in range(0, n, PANEL):
        end = base + PANEL
        part = work[base:end, :]
        pivots = jnp.zeros((PANEL, 1), jnp.float32)
        for j in range(PANEL):
            pivot_row = part[j : j + 1, :]
            pivot = pivot_row[:, base + j : base + j + 1]
            pivots = jnp.where(inside == j, pivot, pivots)
            if j + 1 < PANEL:
                below = jnp.where(inside > j, part[:, base + j : base + j + 1] * (1.0 / pivot), 0.0)
                part = part - below * pivot_row
        part = part * (1.0 / jnp.sqrt(pivots))
        work[base:end, :] = part
        if end < n:
            work[end:, :] -= lax.dot_general(
                part[:, end:n],
                part,
                (((0,), (0,)), ((), ())),
                precision=HIGHEST,
                preferred_element_type=jnp.float32,
            )
    factor[...] = jnp.where(column >= row, work[:, :n], 0.0)
    inverse = work[:, n:]
    piece = 4 * n
    for i in range(sampled.shape[0] // piece):
        rows = pl.ds(i * piece, piece)
        basis[rows, :] = lax.dot_general(
            sampled[rows, :],
            inverse,
            (((1,), (1,)), ((), ())),
            precision=HIGHEST,
            preferred_element_type=jnp.float32,
        )


def finish(order, gram, sampled):
    n = gram.shape[0]
    return pl.pallas_call(
        lambda *refs: finish_kernel(order, *refs),
        out_shape=(
            jax.ShapeDtypeStruct(sampled.shape, jnp.float32),
            jax.ShapeDtypeStruct(gram.shape, jnp.float32),
        ),
        scratch_shapes=[pltpu.VMEM((n, 2 * n), jnp.float32)],
        compiler_params=pltpu.CompilerParams(vmem_limit_bytes=SMALL_VMEM),
        name="finish",
    )(gram, sampled)


def swap(value, axes, mask, size):
    return lax.ppermute(value, axes, [(i, i ^ mask) for i in range(size)])


def sum_four(value, axes, low, high, size):
    others = [swap(value, axes, m, size) for m in (low, high, low ^ high)]
    return (value + others[0]) + (others[1] + others[2])


def shards(tiles, tile_row, tile_owner, tile_offset, counts, sketch):
    row_count = lax.axis_size("row")
    col_count = lax.axis_size("col")
    slot_count, side = tiles.shape[1:3]
    width = sketch.shape[1]
    blocks = sketch.shape[0] // side
    place = lax.axis_index("col")
    core, chip = place % 2, place // 2
    live = counts[0]
    omega, table, early = gather_rows(sketch, side)
    tile_row, tile_owner, tile_offset, _ = lax.optimization_barrier((tile_row, tile_owner, tile_offset, early))
    rows = jnp.where(jnp.arange(slot_count, dtype=jnp.int32) < live, tile_row[0], col_count * blocks)
    order, starts, where, groups = plan(tile_owner[0, :, 0], tile_offset[0], live, table, len(omega), blocks)
    meta = jnp.stack([groups, core]).astype(jnp.int32)
    keep, send = products(tiles[0], omega, order, starts, where, rows, meta, col_count // 2, blocks)

    received = swap(send, "col", 1, col_count)
    others = []
    for k in (2, 1, 3):
        coded = half_sum((chip ^ k).reshape(1), keep, received)
        others.append(swap(coded, "col", 2 * k, col_count))
    sampled, local_gram = total_sum(chip.reshape(1), keep, received, others)

    both = ("row", "col")
    devices = row_count * col_count
    gram = sum_four(local_gram, both, 1, 4 * col_count, devices)
    gram = sum_four(gram, both, 2, 4, devices)
    gram = sum_four(gram, both, col_count, 2 * col_count, devices)
    gram = sum_four(gram, both, 8 * col_count, 16 * col_count, devices)
    return finish(sampled.shape[0] * devices, gram, sampled)


def solution(mesh):
    in_specs = (
        P(("row", "col"), None, None, None),
        P(("row", "col"), None),
        P(("row", "col"), None, None),
        P(("row", "col"), None),
        P(("row", "col")),
        P(("col", "row"), None),
    )
    out_specs = (P(("row", "col"), None), P())
    return jax.shard_map(shards, mesh=mesh, in_specs=in_specs, out_specs=out_specs, check_vma=False)
```

```python
import jax
import jax.numpy as jnp
import numpy as np
from jax import lax
from jax.experimental import pallas as pl
from jax.experimental.pallas import tpu as pltpu
from jax.sharding import PartitionSpec as P

GROUP = 8
VMEM = 60 * 1024 * 1024
SMALL_VMEM = 40 * 1024 * 1024
PANEL = 32
Y_SIZE = 4
Z_SIZE = 8
FIRST_SHARE = 10
HIGHEST = lax.Precision.HIGHEST


def encode(value):
    top = jnp.max(jnp.abs(value), axis=0, keepdims=True)
    top = jnp.maximum(top, 1e-28) * 1.0001
    power = jnp.floor(jnp.log2(top)) - 14.0
    scaled = jnp.round(value * jnp.exp2(-power))
    coded = jnp.clip(scaled, -32767.0, 32767.0).astype(jnp.int32).astype(jnp.int16)
    return coded, power


def encode_block(get_tile, coded_ref, side, count):
    powers = jnp.zeros((count, side), jnp.float32)
    which = lax.broadcasted_iota(jnp.int32, (count, side), 0)

    def one(t, powers):
        coded, power = encode(get_tile(t))
        coded_ref[pl.ds(pl.multiple_of(t * side, side), side), :] = coded
        return jnp.where(which == t, power, powers)

    powers = lax.fori_loop(0, count, one, powers, unroll=2)
    coded_ref[pl.ds(count * side, count), :] = powers.astype(jnp.int32).astype(jnp.int16)


def decode_scales(coded_ref, side, count):
    return jnp.exp2(coded_ref[pl.ds(count * side, count), :].astype(jnp.int32).astype(jnp.float32))


class Piece:
    def __init__(self, array, runs):
        self.array = array
        self.runs = runs

    @property
    def blocks(self):
        return sum(run[3] for run in self.runs)


def cut(piece, first, count, side):
    runs, at = [], 0
    for y, z, start, blocks in piece.runs:
        low, high = max(first, at), min(first + count, at + blocks)
        if high > low:
            runs.append((y, z, start + low - at, high - low))
        at += blocks
    return Piece(piece.array[first * side : (first + count) * side], runs)


def join(pieces):
    return Piece(jnp.concatenate([p.array for p in pieces], 0), [r for p in pieces for r in p.runs])


def shift(piece, dy, dz, after=()):
    array = piece.array
    if after:
        array = lax.optimization_barrier((array,) + tuple(p.array for p in after))[0]
    pairs = [
        (y * Z_SIZE + z, (y + dy) % Y_SIZE * Z_SIZE + (z + dz) % Z_SIZE)
        for y in range(Y_SIZE)
        for z in range(Z_SIZE)
    ]
    runs = [((y - dy) % Y_SIZE, (z - dz) % Z_SIZE, start, n) for y, z, start, n in piece.runs]
    return Piece(lax.ppermute(array, "row", pairs), runs)


def gather_rows(sketch, side):
    def both_y(up, down, after=()):
        return shift(up, 1, 0, after), shift(down, -1, 0, after)

    def both_z(up, down, after=()):
        return shift(up, 0, 1, after), shift(down, 0, -1, after)

    def halves(pair):
        half = pair[0].blocks // 2
        return cut(pair[0], 0, half, side), cut(pair[1], half, pair[1].blocks - half, side)

    blocks = sketch.shape[0] // side
    a = Piece(sketch[: FIRST_SHARE * side], [(0, 0, 0, FIRST_SHARE)])
    b = Piece(sketch[FIRST_SHARE * side :], [(0, 0, FIRST_SHARE, blocks - FIRST_SHARE)])
    za1 = both_z(a, a)
    yb = both_y(b, b)
    ya = both_y(a, a)
    za2 = both_z(*za1)
    yb2 = both_y(*halves(yb))
    za3 = both_z(*za2, after=yb)
    ya2 = both_y(*halves(ya), after=yb)
    p1 = join(za1)
    y1 = both_y(p1, p1, after=ya2)
    around = join([b, *yb, *yb2])
    zb1 = both_z(around, around, after=za2)
    z4 = both_z(*halves(za3), after=ya2)
    p2 = join(za2)
    y2 = both_y(p2, p2, after=za3)
    zb2 = both_z(*zb1, after=y1 + z4)
    p3 = join(za3)
    y3 = both_y(p3, p3, after=y1)
    h1, h2 = halves(y1), halves(y2)
    f1 = both_y(join([h1[0], h2[0], *z4]), join([h1[1], h2[1], *z4]), after=zb1)
    zb3 = both_z(*zb2, after=y3)
    h3, last, first = halves(y3), z4[0].blocks + z4[1].blocks, h1[0].blocks + h2[0].blocks
    half = last // 2
    f2 = both_y(
        join([h3[0], cut(f1[0], first, half, side)]),
        join([h3[1], cut(f1[1], first + half, last - half, side)]),
        after=zb3,
    )
    zb4 = both_z(*halves(zb3), after=f1)
    pieces = [a, *ya, *ya2, p1, *y1, p2, *y2, p3, *y3, *z4, *f1, *f2, around, *zb1, *zb2, *zb3, *zb4]
    table = np.full((Y_SIZE * Z_SIZE * blocks, 2), -1, np.int32)
    for number, piece in enumerate(pieces):
        at = 0
        for y, z, start, count in piece.runs:
            for i in range(count):
                table[(y * Z_SIZE + z) * blocks + start + i] = (number, at)
                at += 1
    assert (table >= 0).all() and sum(p.blocks for p in pieces) == len(table)
    arrays = [p.array.reshape(p.blocks, side, sketch.shape[1]) for p in pieces]
    return arrays, table, yb[0].array


def products_kernel(count, order, starts, place, rows, meta, tiles, *refs):
    omega, (keep, send, tile_buf, omega_buf, total, coded) = refs[:count], refs[count : count + 6]
    tile_sem, omega_sem, keep_sem, send_sem = refs[count + 6 :]
    groups = meta[0]
    core = meta[1]
    side = tiles.shape[1]
    halves = keep.shape[0]
    blocks = (total.shape[0] - 1) // (2 * halves)

    def tile_copy(group):
        part = pl.ds(group * GROUP, GROUP)
        return pltpu.make_async_copy(tiles.at[part], tile_buf.at[part], tile_sem.at[group])

    def fetch_tiles(group, _):
        tile_copy(group).start()
        return 0

    lax.fori_loop(0, groups, fetch_tiles, 0)
    for p in range(count):

        def fetch(j, _, p=p):
            slot = order[j]
            pltpu.make_async_copy(
                omega[p].at[place[slot]], omega_buf.at[slot], omega_sem.at[slot // GROUP]
            ).start()
            return 0

        lax.fori_loop(starts[p], starts[p + 1], fetch, 0)

    def clear(t, _):
        total[t] = jnp.zeros(total.shape[1:], jnp.float32)
        return 0

    lax.fori_loop(0, total.shape[0], clear, 0)

    def step(group, _):
        first = group * GROUP
        tile_copy(group).wait()
        pltpu.make_async_copy(
            tiles.at[pl.ds(0, GROUP)], omega_buf.at[pl.ds(first, GROUP)], omega_sem.at[group]
        ).wait()
        parts = [
            jnp.dot(tile_buf[first + i], omega_buf[first + i], preferred_element_type=jnp.float32)
            for i in range(GROUP)
        ]
        for i in range(GROUP):
            total[rows[first + i]] += parts[i]
        return 0

    lax.fori_loop(0, groups, step, 0)

    def keep_copy(x):
        return pltpu.make_async_copy(
            total.at[pl.ds((2 * x + core) * blocks, blocks)], keep.at[x], keep_sem.at[x]
        )

    def send_copy(x):
        return pltpu.make_async_copy(coded.at[x], send.at[x], send_sem.at[x])

    for x in range(halves):
        keep_copy(x).start()
    for x in range(halves):
        first = (2 * x + 1 - core) * blocks
        encode_block(lambda t: total[first + t], coded.at[x], side, blocks)
        send_copy(x).start()
    for x in range(halves):
        keep_copy(x).wait()
        send_copy(x).wait()


def products(tiles, omega, order, starts, place, rows, meta, halves, blocks):
    slots, side, _ = tiles.shape
    width = omega[0].shape[2]
    panel = 2 * halves * blocks
    any_spec = pl.BlockSpec(memory_space=pl.ANY)
    return pl.pallas_call(
        lambda *refs: products_kernel(len(omega), *refs),
        out_shape=(
            jax.ShapeDtypeStruct((halves, blocks, side, width), jnp.float32),
            jax.ShapeDtypeStruct((halves, blocks * side + blocks, width), jnp.int16),
        ),
        grid_spec=pltpu.PrefetchScalarGridSpec(
            num_scalar_prefetch=5,
            grid=(1,),
            in_specs=[any_spec] * (1 + len(omega)),
            out_specs=(any_spec, any_spec),
            scratch_shapes=[
                pltpu.VMEM((slots, side, side), jnp.bfloat16),
                pltpu.VMEM((slots, side, width), jnp.bfloat16),
                pltpu.VMEM((panel + 1, side, width), jnp.float32),
                pltpu.VMEM((halves, blocks * side + blocks, width), jnp.int16),
                pltpu.SemaphoreType.DMA((slots // GROUP,)),
                pltpu.SemaphoreType.DMA((slots // GROUP,)),
                pltpu.SemaphoreType.DMA((halves,)),
                pltpu.SemaphoreType.DMA((halves,)),
            ],
        ),
        compiler_params=pltpu.CompilerParams(vmem_limit_bytes=VMEM),
        cost_estimate=pl.CostEstimate(flops=2 * slots * side**3, bytes_accessed=24 << 20, transcendentals=0),
        name="products",
    )(order, starts, place, rows, meta, tiles, *omega)


def plan(owner, offset, live, table, pieces, blocks):
    slots = owner.shape[0]
    here = lax.axis_index("row")
    y = (owner // Z_SIZE - here // Z_SIZE) % Y_SIZE
    z = (owner % Z_SIZE - here % Z_SIZE) % Z_SIZE
    code = (y * Z_SIZE + z) * blocks + offset
    chosen = code[:, None] == jnp.arange(len(table), dtype=jnp.int32)[None, :]
    piece = jnp.sum(jnp.where(chosen, jnp.asarray(table[:, 0])[None, :], 0), 1)
    place = jnp.sum(jnp.where(chosen, jnp.asarray(table[:, 1])[None, :], 0), 1)
    groups = (live + GROUP - 1) // GROUP
    number = jnp.arange(slots, dtype=jnp.int32)
    key = jnp.where(number < groups * GROUP, piece, pieces)
    key = key * slots + number
    rank = jnp.sum((key[None, :] < key[:, None]).astype(jnp.int32), 1)
    order = jnp.sum(jnp.where(rank[None, :] == number[:, None], number[None, :], 0), 1)
    limits = jnp.arange(pieces + 1, dtype=jnp.int32) * slots
    starts = jnp.sum((key[None, :] < limits[:, None]).astype(jnp.int32), 1)
    return order, starts, place, groups


def half_sum_kernel(index, keep, received, coded):
    blocks, side = keep.shape[1:3]
    scales = decode_scales(received.at[0], side, blocks)
    which = lax.broadcasted_iota(jnp.int32, scales.shape, 0)

    def tile(t):
        scale = jnp.sum(jnp.where(which == t, scales, 0.0), axis=0, keepdims=True)
        rows = received[0, pl.ds(pl.multiple_of(t * side, side), side), :]
        return keep[0, t] + rows.astype(jnp.int32).astype(jnp.float32) * scale

    encode_block(tile, coded, side, blocks)


def half_sum(index, keep, received):
    _, blocks, side, width = keep.shape
    length = received.shape[1]
    return pl.pallas_call(
        half_sum_kernel,
        out_shape=jax.ShapeDtypeStruct((length, width), jnp.int16),
        grid_spec=pltpu.PrefetchScalarGridSpec(
            num_scalar_prefetch=1,
            grid=(1,),
            in_specs=[
                pl.BlockSpec((1, blocks, side, width), lambda i, index: (index[0], 0, 0, 0)),
                pl.BlockSpec((1, length, width), lambda i, index: (index[0], 0, 0)),
            ],
            out_specs=pl.BlockSpec((length, width), lambda i, index: (0, 0)),
        ),
        compiler_params=pltpu.CompilerParams(vmem_limit_bytes=SMALL_VMEM),
        cost_estimate=pl.CostEstimate(flops=1 << 22, bytes_accessed=2 << 20, transcendentals=0),
        name="half_sum",
    )(index, keep, received)


def total_kernel(index, keep, received, first, second, third, sampled, gram):
    blocks, side = keep.shape[1:3]
    parts = [received.at[0], first, second, third]
    scales = [decode_scales(p, side, blocks) for p in parts]
    which = lax.broadcasted_iota(jnp.int32, scales[0].shape, 0)

    def tile(t, _):
        rows = pl.ds(pl.multiple_of(t * side, side), side)
        terms = [keep[0, t]]
        for p, s in zip(parts, scales):
            scale = jnp.sum(jnp.where(which == t, s, 0.0), axis=0, keepdims=True)
            terms.append(p[rows, :].astype(jnp.int32).astype(jnp.float32) * scale)
        sampled[rows, :] = (terms[0] + terms[1]) + (terms[2] + terms[3]) + terms[4]
        return 0

    lax.fori_loop(0, blocks, tile, 0)
    piece = 4 * side
    acc = None
    for i in range(blocks // 4):
        part = sampled[pl.ds(i * piece, piece), :]
        term = lax.dot_general(
            part, part, (((0,), (0,)), ((), ())), precision=HIGHEST, preferred_element_type=jnp.float32
        )
        acc = term if acc is None else acc + term
    gram[...] = acc


def total_sum(index, keep, received, others):
    _, blocks, side, width = keep.shape
    length = received.shape[1]
    whole = pl.BlockSpec((length, width), lambda i, index: (0, 0))
    return pl.pallas_call(
        total_kernel,
        out_shape=(
            jax.ShapeDtypeStruct((blocks * side, width), jnp.float32),
            jax.ShapeDtypeStruct((width, width), jnp.float32),
        ),
        grid_spec=pltpu.PrefetchScalarGridSpec(
            num_scalar_prefetch=1,
            grid=(1,),
            in_specs=[
                pl.BlockSpec((1, blocks, side, width), lambda i, index: (index[0], 0, 0, 0)),
                pl.BlockSpec((1, length, width), lambda i, index: (index[0], 0, 0)),
                whole,
                whole,
                whole,
            ],
            out_specs=(
                pl.BlockSpec((blocks * side, width), lambda i, index: (0, 0)),
                pl.BlockSpec((width, width), lambda i, index: (0, 0)),
            ),
        ),
        compiler_params=pltpu.CompilerParams(vmem_limit_bytes=SMALL_VMEM),
        name="total_sum",
    )(index, keep, received, *others)


def finish_kernel(order, gram, sampled, basis, factor, work):
    n = gram.shape[0]
    row = lax.broadcasted_iota(jnp.int32, (n, n), 0)
    column = lax.broadcasted_iota(jnp.int32, (n, n), 1)
    work[:, :n] = gram[...] * (1.0 / order)
    work[:, n:] = jnp.where(row == column, 1.0, 0.0)
    inside = lax.broadcasted_iota(jnp.int32, (PANEL, 1), 0)
    for base in range(0, n, PANEL):
        end = base + PANEL
        part = work[base:end, :]
        pivots = jnp.zeros((PANEL, 1), jnp.float32)
        for j in range(PANEL):
            pivot_row = part[j : j + 1, :]
            pivot = pivot_row[:, base + j : base + j + 1]
            pivots = jnp.where(inside == j, pivot, pivots)
            if j + 1 < PANEL:
                below = jnp.where(inside > j, part[:, base + j : base + j + 1] * (1.0 / pivot), 0.0)
                part = part - below * pivot_row
        part = part * (1.0 / jnp.sqrt(pivots))
        work[base:end, :] = part
        if end < n:
            work[end:, :] -= lax.dot_general(
                part[:, end:n],
                part,
                (((0,), (0,)), ((), ())),
                precision=HIGHEST,
                preferred_element_type=jnp.float32,
            )
    factor[...] = jnp.where(column >= row, work[:, :n], 0.0)
    inverse = work[:, n:]
    piece = 4 * n
    for i in range(sampled.shape[0] // piece):
        rows = pl.ds(i * piece, piece)
        basis[rows, :] = lax.dot_general(
            sampled[rows, :],
            inverse,
            (((1,), (1,)), ((), ())),
            precision=HIGHEST,
            preferred_element_type=jnp.float32,
        )


def finish(order, gram, sampled):
    n = gram.shape[0]
    return pl.pallas_call(
        lambda *refs: finish_kernel(order, *refs),
        out_shape=(
            jax.ShapeDtypeStruct(sampled.shape, jnp.float32),
            jax.ShapeDtypeStruct(gram.shape, jnp.float32),
        ),
        scratch_shapes=[pltpu.VMEM((n, 2 * n), jnp.float32)],
        compiler_params=pltpu.CompilerParams(vmem_limit_bytes=SMALL_VMEM),
        name="finish",
    )(gram, sampled)


def swap(value, axes, mask, size):
    return lax.ppermute(value, axes, [(i, i ^ mask) for i in range(size)])


def sum_four(value, axes, low, high, size):
    others = [swap(value, axes, m, size) for m in (low, high, low ^ high)]
    return (value + others[0]) + (others[1] + others[2])


def shards(tiles, tile_row, tile_owner, tile_offset, counts, sketch):
    row_count = lax.axis_size("row")
    col_count = lax.axis_size("col")
    slot_count, side = tiles.shape[1:3]
    width = sketch.shape[1]
    blocks = sketch.shape[0] // side
    place = lax.axis_index("col")
    core, chip = place % 2, place // 2
    live = counts[0]
    omega, table, early = gather_rows(sketch, side)
    tile_row, tile_owner, tile_offset, _ = lax.optimization_barrier((tile_row, tile_owner, tile_offset, early))
    rows = jnp.where(jnp.arange(slot_count, dtype=jnp.int32) < live, tile_row[0], col_count * blocks)
    order, starts, where, groups = plan(tile_owner[0, :, 0], tile_offset[0], live, table, len(omega), blocks)
    meta = jnp.stack([groups, core]).astype(jnp.int32)
    keep, send = products(tiles[0], omega, order, starts, where, rows, meta, col_count // 2, blocks)

    received = swap(send, "col", 1, col_count)
    others = []
    for k in (2, 1, 3):
        coded = half_sum((chip ^ k).reshape(1), keep, received)
        others.append(swap(coded, "col", 2 * k, col_count))
    sampled, local_gram = total_sum(chip.reshape(1), keep, received, others)

    both = ("row", "col")
    devices = row_count * col_count
    gram = sum_four(local_gram, both, 1, 4 * col_count, devices)
    gram = sum_four(gram, both, 2, 4, devices)
    gram = sum_four(gram, both, col_count, 2 * col_count, devices)
    gram = sum_four(gram, both, 8 * col_count, 16 * col_count, devices)
    return finish(sampled.shape[0] * devices, gram, sampled)


def solution(mesh):
    in_specs = (
        P(("row", "col"), None, None, None),
        P(("row", "col"), None),
        P(("row", "col"), None, None),
        P(("row", "col"), None),
        P(("row", "col")),
        P(("col", "row"), None),
    )
    out_specs = (P(("row", "col"), None), P())
    return jax.shard_map(shards, mesh=mesh, in_specs=in_specs, out_specs=out_specs, check_vma=False)
```

```python
import jax
import jax.numpy as jnp
import numpy as np
from jax import lax
from jax.experimental import pallas as pl
from jax.experimental.pallas import tpu as pltpu
from jax.sharding import PartitionSpec as P

GROUP = 8
VMEM = 60 * 1024 * 1024
SMALL_VMEM = 40 * 1024 * 1024
PANEL = 32
Y_SIZE = 4
Z_SIZE = 8
FIRST_SHARE = 10
HIGHEST = lax.Precision.HIGHEST


def encode(value):
    top = jnp.max(jnp.abs(value), axis=0, keepdims=True)
    top = jnp.maximum(top, 1e-28) * 1.0001
    power = jnp.floor(jnp.log2(top)) - 14.0
    scaled = jnp.round(value * jnp.exp2(-power))
    coded = jnp.clip(scaled, -32767.0, 32767.0).astype(jnp.int32).astype(jnp.int16)
    return coded, power


def encode_block(get_tile, coded_ref, side, count):
    powers = jnp.zeros((count, side), jnp.float32)
    which = lax.broadcasted_iota(jnp.int32, (count, side), 0)

    def one(t, powers):
        coded, power = encode(get_tile(t))
        coded_ref[pl.ds(pl.multiple_of(t * side, side), side), :] = coded
        return jnp.where(which == t, power, powers)

    powers = lax.fori_loop(0, count, one, powers, unroll=2)
    coded_ref[pl.ds(count * side, count), :] = powers.astype(jnp.int32).astype(jnp.int16)


def decode_scales(coded_ref, side, count):
    return jnp.exp2(coded_ref[pl.ds(count * side, count), :].astype(jnp.int32).astype(jnp.float32))


class Piece:
    def __init__(self, array, runs):
        self.array = array
        self.runs = runs

    @property
    def blocks(self):
        return sum(run[3] for run in self.runs)


def cut(piece, first, count, side):
    runs, at = [], 0
    for y, z, start, blocks in piece.runs:
        low, high = max(first, at), min(first + count, at + blocks)
        if high > low:
            runs.append((y, z, start + low - at, high - low))
        at += blocks
    return Piece(piece.array[first * side : (first + count) * side], runs)


def join(pieces):
    return Piece(jnp.concatenate([p.array for p in pieces], 0), [r for p in pieces for r in p.runs])


def shift(piece, dy, dz, after=()):
    array = piece.array
    if after:
        array = lax.optimization_barrier((array,) + tuple(p.array for p in after))[0]
    pairs = [
        (y * Z_SIZE + z, (y + dy) % Y_SIZE * Z_SIZE + (z + dz) % Z_SIZE)
        for y in range(Y_SIZE)
        for z in range(Z_SIZE)
    ]
    runs = [((y - dy) % Y_SIZE, (z - dz) % Z_SIZE, start, n) for y, z, start, n in piece.runs]
    return Piece(lax.ppermute(array, "row", pairs), runs)


def gather_rows(sketch, side):
    def both_y(up, down, after=()):
        return shift(up, 1, 0, after), shift(down, -1, 0, after)

    def both_z(up, down, after=()):
        return shift(up, 0, 1, after), shift(down, 0, -1, after)

    def halves(pair):
        half = pair[0].blocks // 2
        return cut(pair[0], 0, half, side), cut(pair[1], half, pair[1].blocks - half, side)

    blocks = sketch.shape[0] // side
    a = Piece(sketch[: FIRST_SHARE * side], [(0, 0, 0, FIRST_SHARE)])
    b = Piece(sketch[FIRST_SHARE * side :], [(0, 0, FIRST_SHARE, blocks - FIRST_SHARE)])
    za1 = both_z(a, a)
    yb = both_y(b, b)
    ya = both_y(a, a)
    za2 = both_z(*za1)
    yb2 = both_y(*halves(yb))
    za3 = both_z(*za2, after=yb)
    ya2 = both_y(*halves(ya), after=yb)
    p1 = join(za1)
    y1 = both_y(p1, p1, after=ya2)
    around = join([b, *yb, *yb2])
    zb1 = both_z(around, around, after=za2)
    z4 = (shift(za3[0], 0, 1, ya2),)
    p2 = join(za2)
    y2 = both_y(p2, p2, after=za3)
    zb2 = both_z(*zb1, after=y1 + z4)
    p3 = join(za3)
    y3 = both_y(p3, p3, after=y1)
    h1, h2 = halves(y1), halves(y2)
    f1 = both_y(join([h1[0], h2[0], *z4]), join([h1[1], h2[1], *z4]), after=zb1)
    zb3 = both_z(*zb2, after=y3)
    h3, last, first = halves(y3), z4[0].blocks, h1[0].blocks + h2[0].blocks
    half = last // 2
    f2 = both_y(
        join([h3[0], cut(f1[0], first, half, side)]),
        join([h3[1], cut(f1[1], first + half, last - half, side)]),
        after=zb3,
    )
    zb4 = both_z(*halves(zb3), after=f1)
    pieces = [a, *ya, *ya2, p1, *y1, p2, *y2, p3, *y3, *z4, *f1, *f2, around, *zb1, *zb2, *zb3, *zb4]
    table = np.full((Y_SIZE * Z_SIZE * blocks, 2), -1, np.int32)
    for number, piece in enumerate(pieces):
        at = 0
        for y, z, start, count in piece.runs:
            for i in range(count):
                table[(y * Z_SIZE + z) * blocks + start + i] = (number, at)
                at += 1
    assert (table >= 0).all() and sum(p.blocks for p in pieces) == len(table)
    arrays = [p.array.reshape(p.blocks, side, sketch.shape[1]) for p in pieces]
    return arrays, table, yb[0].array


def products_kernel(count, order, starts, place, rows, meta, tiles, *refs):
    omega, (keep, send, tile_buf, omega_buf, total, coded) = refs[:count], refs[count : count + 6]
    tile_sem, omega_sem, keep_sem, send_sem = refs[count + 6 :]
    groups = meta[0]
    core = meta[1]
    side = tiles.shape[1]
    halves = keep.shape[0]
    blocks = (total.shape[0] - 1) // (2 * halves)

    def tile_copy(group):
        part = pl.ds(group * GROUP, GROUP)
        return pltpu.make_async_copy(tiles.at[part], tile_buf.at[part], tile_sem.at[group])

    def fetch_tiles(group, _):
        tile_copy(group).start()
        return 0

    lax.fori_loop(0, groups, fetch_tiles, 0)
    for p in range(count):

        def fetch(j, _, p=p):
            slot = order[j]
            pltpu.make_async_copy(
                omega[p].at[place[slot]], omega_buf.at[slot], omega_sem.at[slot // GROUP]
            ).start()
            return 0

        lax.fori_loop(starts[p], starts[p + 1], fetch, 0)

    def clear(t, _):
        total[t] = jnp.zeros(total.shape[1:], jnp.float32)
        return 0

    lax.fori_loop(0, total.shape[0], clear, 0)

    def step(group, _):
        first = group * GROUP
        tile_copy(group).wait()
        pltpu.make_async_copy(
            tiles.at[pl.ds(0, GROUP)], omega_buf.at[pl.ds(first, GROUP)], omega_sem.at[group]
        ).wait()
        parts = [
            jnp.dot(tile_buf[first + i], omega_buf[first + i], preferred_element_type=jnp.float32)
            for i in range(GROUP)
        ]
        for i in range(GROUP):
            total[rows[first + i]] += parts[i]
        return 0

    lax.fori_loop(0, groups, step, 0)

    def keep_copy(x):
        return pltpu.make_async_copy(
            total.at[pl.ds((2 * x + core) * blocks, blocks)], keep.at[x], keep_sem.at[x]
        )

    def send_copy(x):
        return pltpu.make_async_copy(coded.at[x], send.at[x], send_sem.at[x])

    for x in range(halves):
        keep_copy(x).start()
    for x in range(halves):
        first = (2 * x + 1 - core) * blocks
        encode_block(lambda t: total[first + t], coded.at[x], side, blocks)
        send_copy(x).start()
    for x in range(halves):
        keep_copy(x).wait()
        send_copy(x).wait()


def products(tiles, omega, order, starts, place, rows, meta, halves, blocks):
    slots, side, _ = tiles.shape
    width = omega[0].shape[2]
    panel = 2 * halves * blocks
    any_spec = pl.BlockSpec(memory_space=pl.ANY)
    return pl.pallas_call(
        lambda *refs: products_kernel(len(omega), *refs),
        out_shape=(
            jax.ShapeDtypeStruct((halves, blocks, side, width), jnp.float32),
            jax.ShapeDtypeStruct((halves, blocks * side + blocks, width), jnp.int16),
        ),
        grid_spec=pltpu.PrefetchScalarGridSpec(
            num_scalar_prefetch=5,
            grid=(1,),
            in_specs=[any_spec] * (1 + len(omega)),
            out_specs=(any_spec, any_spec),
            scratch_shapes=[
                pltpu.VMEM((slots, side, side), jnp.bfloat16),
                pltpu.VMEM((slots, side, width), jnp.bfloat16),
                pltpu.VMEM((panel + 1, side, width), jnp.float32),
                pltpu.VMEM((halves, blocks * side + blocks, width), jnp.int16),
                pltpu.SemaphoreType.DMA((slots // GROUP,)),
                pltpu.SemaphoreType.DMA((slots // GROUP,)),
                pltpu.SemaphoreType.DMA((halves,)),
                pltpu.SemaphoreType.DMA((halves,)),
            ],
        ),
        compiler_params=pltpu.CompilerParams(vmem_limit_bytes=VMEM),
        cost_estimate=pl.CostEstimate(flops=2 * slots * side**3, bytes_accessed=24 << 20, transcendentals=0),
        name="products",
    )(order, starts, place, rows, meta, tiles, *omega)


def plan(owner, offset, live, table, pieces, blocks):
    slots = owner.shape[0]
    here = lax.axis_index("row")
    y = (owner // Z_SIZE - here // Z_SIZE) % Y_SIZE
    z = (owner % Z_SIZE - here % Z_SIZE) % Z_SIZE
    code = (y * Z_SIZE + z) * blocks + offset
    chosen = code[:, None] == jnp.arange(len(table), dtype=jnp.int32)[None, :]
    piece = jnp.sum(jnp.where(chosen, jnp.asarray(table[:, 0])[None, :], 0), 1)
    place = jnp.sum(jnp.where(chosen, jnp.asarray(table[:, 1])[None, :], 0), 1)
    groups = (live + GROUP - 1) // GROUP
    number = jnp.arange(slots, dtype=jnp.int32)
    key = jnp.where(number < groups * GROUP, piece, pieces)
    key = key * slots + number
    rank = jnp.sum((key[None, :] < key[:, None]).astype(jnp.int32), 1)
    order = jnp.sum(jnp.where(rank[None, :] == number[:, None], number[None, :], 0), 1)
    limits = jnp.arange(pieces + 1, dtype=jnp.int32) * slots
    starts = jnp.sum((key[None, :] < limits[:, None]).astype(jnp.int32), 1)
    return order, starts, place, groups


def half_sum_kernel(index, keep, received, coded):
    blocks, side = keep.shape[1:3]
    scales = decode_scales(received.at[0], side, blocks)
    which = lax.broadcasted_iota(jnp.int32, scales.shape, 0)

    def tile(t):
        scale = jnp.sum(jnp.where(which == t, scales, 0.0), axis=0, keepdims=True)
        rows = received[0, pl.ds(pl.multiple_of(t * side, side), side), :]
        return keep[0, t] + rows.astype(jnp.int32).astype(jnp.float32) * scale

    encode_block(tile, coded, side, blocks)


def half_sum(index, keep, received):
    _, blocks, side, width = keep.shape
    length = received.shape[1]
    return pl.pallas_call(
        half_sum_kernel,
        out_shape=jax.ShapeDtypeStruct((length, width), jnp.int16),
        grid_spec=pltpu.PrefetchScalarGridSpec(
            num_scalar_prefetch=1,
            grid=(1,),
            in_specs=[
                pl.BlockSpec((1, blocks, side, width), lambda i, index: (index[0], 0, 0, 0)),
                pl.BlockSpec((1, length, width), lambda i, index: (index[0], 0, 0)),
            ],
            out_specs=pl.BlockSpec((length, width), lambda i, index: (0, 0)),
        ),
        compiler_params=pltpu.CompilerParams(vmem_limit_bytes=SMALL_VMEM),
        cost_estimate=pl.CostEstimate(flops=1 << 22, bytes_accessed=2 << 20, transcendentals=0),
        name="half_sum",
    )(index, keep, received)


def total_kernel(index, keep, received, first, second, third, sampled, gram):
    blocks, side = keep.shape[1:3]
    parts = [received.at[0], first, second, third]
    scales = [decode_scales(p, side, blocks) for p in parts]
    which = lax.broadcasted_iota(jnp.int32, scales[0].shape, 0)

    def tile(t, _):
        rows = pl.ds(pl.multiple_of(t * side, side), side)
        terms = [keep[0, t]]
        for p, s in zip(parts, scales):
            scale = jnp.sum(jnp.where(which == t, s, 0.0), axis=0, keepdims=True)
            terms.append(p[rows, :].astype(jnp.int32).astype(jnp.float32) * scale)
        sampled[rows, :] = (terms[0] + terms[1]) + (terms[2] + terms[3]) + terms[4]
        return 0

    lax.fori_loop(0, blocks, tile, 0)
    piece = 4 * side
    acc = None
    for i in range(blocks // 4):
        part = sampled[pl.ds(i * piece, piece), :]
        term = lax.dot_general(
            part, part, (((0,), (0,)), ((), ())), precision=HIGHEST, preferred_element_type=jnp.float32
        )
        acc = term if acc is None else acc + term
    gram[...] = acc


def total_sum(index, keep, received, others):
    _, blocks, side, width = keep.shape
    length = received.shape[1]
    whole = pl.BlockSpec((length, width), lambda i, index: (0, 0))
    return pl.pallas_call(
        total_kernel,
        out_shape=(
            jax.ShapeDtypeStruct((blocks * side, width), jnp.float32),
            jax.ShapeDtypeStruct((width, width), jnp.float32),
        ),
        grid_spec=pltpu.PrefetchScalarGridSpec(
            num_scalar_prefetch=1,
            grid=(1,),
            in_specs=[
                pl.BlockSpec((1, blocks, side, width), lambda i, index: (index[0], 0, 0, 0)),
                pl.BlockSpec((1, length, width), lambda i, index: (index[0], 0, 0)),
                whole,
                whole,
                whole,
            ],
            out_specs=(
                pl.BlockSpec((blocks * side, width), lambda i, index: (0, 0)),
                pl.BlockSpec((width, width), lambda i, index: (0, 0)),
            ),
        ),
        compiler_params=pltpu.CompilerParams(vmem_limit_bytes=SMALL_VMEM),
        name="total_sum",
    )(index, keep, received, *others)


def finish_kernel(order, gram, sampled, basis, factor, work):
    n = gram.shape[0]
    row = lax.broadcasted_iota(jnp.int32, (n, n), 0)
    column = lax.broadcasted_iota(jnp.int32, (n, n), 1)
    work[:, :n] = gram[...] * (1.0 / order)
    work[:, n:] = jnp.where(row == column, 1.0, 0.0)
    inside = lax.broadcasted_iota(jnp.int32, (PANEL, 1), 0)
    for base in range(0, n, PANEL):
        end = base + PANEL
        part = work[base:end, :]
        pivots = jnp.zeros((PANEL, 1), jnp.float32)
        for j in range(PANEL):
            pivot_row = part[j : j + 1, :]
            pivot = pivot_row[:, base + j : base + j + 1]
            pivots = jnp.where(inside == j, pivot, pivots)
            if j + 1 < PANEL:
                below = jnp.where(inside > j, part[:, base + j : base + j + 1] * (1.0 / pivot), 0.0)
                part = part - below * pivot_row
        part = part * (1.0 / jnp.sqrt(pivots))
        work[base:end, :] = part
        if end < n:
            work[end:, :] -= lax.dot_general(
                part[:, end:n],
                part,
                (((0,), (0,)), ((), ())),
                precision=HIGHEST,
                preferred_element_type=jnp.float32,
            )
    factor[...] = jnp.where(column >= row, work[:, :n], 0.0)
    inverse = work[:, n:]
    piece = 4 * n
    for i in range(sampled.shape[0] // piece):
        rows = pl.ds(i * piece, piece)
        basis[rows, :] = lax.dot_general(
            sampled[rows, :],
            inverse,
            (((1,), (1,)), ((), ())),
            precision=HIGHEST,
            preferred_element_type=jnp.float32,
        )


def finish(order, gram, sampled):
    n = gram.shape[0]
    return pl.pallas_call(
        lambda *refs: finish_kernel(order, *refs),
        out_shape=(
            jax.ShapeDtypeStruct(sampled.shape, jnp.float32),
            jax.ShapeDtypeStruct(gram.shape, jnp.float32),
        ),
        scratch_shapes=[pltpu.VMEM((n, 2 * n), jnp.float32)],
        compiler_params=pltpu.CompilerParams(vmem_limit_bytes=SMALL_VMEM),
        name="finish",
    )(gram, sampled)


def swap(value, axes, mask, size):
    return lax.ppermute(value, axes, [(i, i ^ mask) for i in range(size)])


def sum_four(value, axes, low, high, size):
    others = [swap(value, axes, m, size) for m in (low, high, low ^ high)]
    return (value + others[0]) + (others[1] + others[2])


def shards(tiles, tile_row, tile_owner, tile_offset, counts, sketch):
    row_count = lax.axis_size("row")
    col_count = lax.axis_size("col")
    slot_count, side = tiles.shape[1:3]
    width = sketch.shape[1]
    blocks = sketch.shape[0] // side
    place = lax.axis_index("col")
    core, chip = place % 2, place // 2
    live = counts[0]
    omega, table, early = gather_rows(sketch, side)
    tile_row, tile_owner, tile_offset, _ = lax.optimization_barrier((tile_row, tile_owner, tile_offset, early))
    rows = jnp.where(jnp.arange(slot_count, dtype=jnp.int32) < live, tile_row[0], col_count * blocks)
    order, starts, where, groups = plan(tile_owner[0, :, 0], tile_offset[0], live, table, len(omega), blocks)
    meta = jnp.stack([groups, core]).astype(jnp.int32)
    keep, send = products(tiles[0], omega, order, starts, where, rows, meta, col_count // 2, blocks)

    received = swap(send, "col", 1, col_count)
    others = []
    for k in (2, 1, 3):
        coded = half_sum((chip ^ k).reshape(1), keep, received)
        others.append(swap(coded, "col", 2 * k, col_count))
    sampled, local_gram = total_sum(chip.reshape(1), keep, received, others)

    both = ("row", "col")
    devices = row_count * col_count
    gram = sum_four(local_gram, both, 1, 4 * col_count, devices)
    gram = sum_four(gram, both, 2, 4, devices)
    gram = sum_four(gram, both, col_count, 2 * col_count, devices)
    gram = sum_four(gram, both, 8 * col_count, 16 * col_count, devices)
    return finish(sampled.shape[0] * devices, gram, sampled)


def solution(mesh):
    in_specs = (
        P(("row", "col"), None, None, None),
        P(("row", "col"), None),
        P(("row", "col"), None, None),
        P(("row", "col"), None),
        P(("row", "col")),
        P(("col", "row"), None),
    )
    out_specs = (P(("row", "col"), None), P())
    return jax.shard_map(shards, mesh=mesh, in_specs=in_specs, out_specs=out_specs, check_vma=False)
```

```python
import jax
import jax.numpy as jnp
import numpy as np
from jax import lax
from jax.experimental import pallas as pl
from jax.experimental.pallas import tpu as pltpu
from jax.sharding import PartitionSpec as P

GROUP = 8
VMEM = 60 * 1024 * 1024
SMALL_VMEM = 40 * 1024 * 1024
PANEL = 32
Y_SIZE = 4
Z_SIZE = 8
FIRST_SHARE = 10
HIGHEST = lax.Precision.HIGHEST


def encode(value):
    top = jnp.max(jnp.abs(value), axis=0, keepdims=True)
    top = jnp.maximum(top, 1e-28) * 1.0001
    power = jnp.floor(jnp.log2(top)) - 14.0
    scaled = jnp.round(value * jnp.exp2(-power))
    coded = jnp.clip(scaled, -32767.0, 32767.0).astype(jnp.int32).astype(jnp.int16)
    return coded, power


def encode_block(get_tile, coded_ref, side, count):
    powers = jnp.zeros((count, side), jnp.float32)
    which = lax.broadcasted_iota(jnp.int32, (count, side), 0)

    def one(t, powers):
        coded, power = encode(get_tile(t))
        coded_ref[pl.ds(pl.multiple_of(t * side, side), side), :] = coded
        return jnp.where(which == t, power, powers)

    powers = lax.fori_loop(0, count, one, powers, unroll=2)
    coded_ref[pl.ds(count * side, count), :] = powers.astype(jnp.int32).astype(jnp.int16)


def decode_scales(coded_ref, side, count):
    return jnp.exp2(coded_ref[pl.ds(count * side, count), :].astype(jnp.int32).astype(jnp.float32))


class Piece:
    def __init__(self, array, runs):
        self.array = array
        self.runs = runs

    @property
    def blocks(self):
        return sum(run[3] for run in self.runs)


def cut(piece, first, count, side):
    runs, at = [], 0
    for y, z, start, blocks in piece.runs:
        low, high = max(first, at), min(first + count, at + blocks)
        if high > low:
            runs.append((y, z, start + low - at, high - low))
        at += blocks
    return Piece(piece.array[first * side : (first + count) * side], runs)


def join(pieces):
    return Piece(jnp.concatenate([p.array for p in pieces], 0), [r for p in pieces for r in p.runs])


def shift(piece, dy, dz, after=()):
    array = piece.array
    if after:
        array = lax.optimization_barrier((array,) + tuple(p.array for p in after))[0]
    pairs = [
        (y * Z_SIZE + z, (y + dy) % Y_SIZE * Z_SIZE + (z + dz) % Z_SIZE)
        for y in range(Y_SIZE)
        for z in range(Z_SIZE)
    ]
    runs = [((y - dy) % Y_SIZE, (z - dz) % Z_SIZE, start, n) for y, z, start, n in piece.runs]
    return Piece(lax.ppermute(array, "row", pairs), runs)


def gather_rows(sketch, side):
    def both_y(up, down, after=()):
        return shift(up, 1, 0, after), shift(down, -1, 0, after)

    def both_z(up, down, after=()):
        return shift(up, 0, 1, after), shift(down, 0, -1, after)

    def halves(pair):
        half = pair[0].blocks // 2
        return cut(pair[0], 0, half, side), cut(pair[1], half, pair[1].blocks - half, side)

    blocks = sketch.shape[0] // side
    a = Piece(sketch[: FIRST_SHARE * side], [(0, 0, 0, FIRST_SHARE)])
    b = Piece(sketch[FIRST_SHARE * side :], [(0, 0, FIRST_SHARE, blocks - FIRST_SHARE)])
    za1 = both_z(a, a)
    yb = both_y(b, b)
    ya = both_y(a, a)
    za2 = both_z(*za1)
    yb2 = both_y(*halves(yb))
    za3 = both_z(*za2, after=yb)
    ya2 = both_y(*halves(ya), after=yb)
    p1 = join(za1)
    y1 = both_y(p1, p1, after=ya2)
    around = join([b, *yb, *yb2])
    zb1 = both_z(around, around, after=za2)
    z4 = (shift(za3[0], 0, 1, ya2),)
    p2 = join(za2)
    y2 = both_y(p2, p2, after=za3)
    zb2 = both_z(*zb1, after=y1 + z4)
    p3 = join(za3)
    y3 = both_y(p3, p3, after=y1)
    h1, h2 = halves(y1), halves(y2)
    f1 = both_y(join([h1[0], h2[0], *z4]), join([h1[1], h2[1], *z4]), after=zb1)
    zb3 = both_z(*zb2, after=y3)
    h3, last, first = halves(y3), z4[0].blocks, h1[0].blocks + h2[0].blocks
    half = last // 2
    f2 = both_y(
        join([h3[0], cut(f1[0], first, half, side)]),
        join([h3[1], cut(f1[1], first + half, last - half, side)]),
        after=zb3,
    )
    zb4 = both_z(*halves(zb3), after=f1)
    pieces = [a, *ya, *ya2, p1, *y1, p2, *y2, p3, *y3, *z4, *f1, *f2, around, *zb1, *zb2, *zb3, *zb4]
    table = np.full((Y_SIZE * Z_SIZE * blocks, 2), -1, np.int32)
    for number, piece in enumerate(pieces):
        at = 0
        for y, z, start, count in piece.runs:
            for i in range(count):
                table[(y * Z_SIZE + z) * blocks + start + i] = (number, at)
                at += 1
    assert (table >= 0).all() and sum(p.blocks for p in pieces) == len(table)
    arrays = [p.array.reshape(p.blocks, side, sketch.shape[1]) for p in pieces]
    return arrays, table, yb[0].array


def products_kernel(count, order, starts, place, rows, meta, tiles, *refs):
    omega, keep, send = refs[:count], refs[count : count + 4], refs[count + 4]
    tile_buf, omega_buf, total, coded, tile_sem, omega_sem, keep_sem, send_sem = refs[count + 5 :]
    groups = meta[0]
    core = meta[1]
    side = tiles.shape[1]
    halves = len(keep)
    blocks = (total.shape[0] - 1) // (2 * halves)

    def tile_copy(group):
        part = pl.ds(group * GROUP, GROUP)
        return pltpu.make_async_copy(tiles.at[part], tile_buf.at[part], tile_sem.at[group])

    def fetch_tiles(group, _):
        tile_copy(group).start()
        return 0

    lax.fori_loop(0, groups, fetch_tiles, 0)
    for p in range(count):

        def fetch(j, _, p=p):
            slot = order[j]
            pltpu.make_async_copy(
                omega[p].at[place[slot]], omega_buf.at[slot], omega_sem.at[slot // GROUP]
            ).start()
            return 0

        lax.fori_loop(starts[p], starts[p + 1], fetch, 0)

    def clear(t, _):
        total[t] = jnp.zeros(total.shape[1:], jnp.float32)
        return 0

    lax.fori_loop(0, total.shape[0], clear, 0)

    def step(group, _):
        first = group * GROUP
        tile_copy(group).wait()
        pltpu.make_async_copy(
            tiles.at[pl.ds(0, GROUP)], omega_buf.at[pl.ds(first, GROUP)], omega_sem.at[group]
        ).wait()
        parts = [
            jnp.dot(tile_buf[first + i], omega_buf[first + i], preferred_element_type=jnp.float32)
            for i in range(GROUP)
        ]
        for i in range(GROUP):
            total[rows[first + i]] += parts[i]
        return 0

    lax.fori_loop(0, groups, step, 0)

    def keep_copy(i):
        first = (2 * meta[2 + i] + core) * blocks
        return pltpu.make_async_copy(total.at[pl.ds(first, blocks)], keep[i], keep_sem.at[i])

    def send_copy(i):
        return pltpu.make_async_copy(coded.at[i], send.at[i], send_sem.at[i])

    for i in range(halves):
        keep_copy(i).start()
    for i in range(halves):
        first = (2 * meta[2 + i] + 1 - core) * blocks
        encode_block(lambda t: total[first + t], coded.at[i], side, blocks)
        send_copy(i).start()
    for i in range(halves):
        keep_copy(i).wait()
        send_copy(i).wait()


def products(tiles, omega, order, starts, place, rows, meta, halves, blocks):
    slots, side, _ = tiles.shape
    width = omega[0].shape[2]
    panel = 2 * halves * blocks
    any_spec = pl.BlockSpec(memory_space=pl.ANY)
    return pl.pallas_call(
        lambda *refs: products_kernel(len(omega), *refs),
        out_shape=(
            *[jax.ShapeDtypeStruct((blocks, side, width), jnp.float32)] * halves,
            jax.ShapeDtypeStruct((halves, blocks * side + blocks, width), jnp.int16),
        ),
        grid_spec=pltpu.PrefetchScalarGridSpec(
            num_scalar_prefetch=5,
            grid=(1,),
            in_specs=[any_spec] * (1 + len(omega)),
            out_specs=(any_spec,) * (halves + 1),
            scratch_shapes=[
                pltpu.VMEM((slots, side, side), jnp.bfloat16),
                pltpu.VMEM((slots, side, width), jnp.bfloat16),
                pltpu.VMEM((panel + 1, side, width), jnp.float32),
                pltpu.VMEM((halves, blocks * side + blocks, width), jnp.int16),
                pltpu.SemaphoreType.DMA((slots // GROUP,)),
                pltpu.SemaphoreType.DMA((slots // GROUP,)),
                pltpu.SemaphoreType.DMA((halves,)),
                pltpu.SemaphoreType.DMA((halves,)),
            ],
        ),
        compiler_params=pltpu.CompilerParams(vmem_limit_bytes=VMEM),
        cost_estimate=pl.CostEstimate(flops=2 * slots * side**3, bytes_accessed=24 << 20, transcendentals=0),
        name="products",
    )(order, starts, place, rows, meta, tiles, *omega)


def plan(owner, offset, live, table, pieces, blocks):
    slots = owner.shape[0]
    here = lax.axis_index("row")
    y = (owner // Z_SIZE - here // Z_SIZE) % Y_SIZE
    z = (owner % Z_SIZE - here % Z_SIZE) % Z_SIZE
    code = (y * Z_SIZE + z) * blocks + offset
    chosen = code[:, None] == jnp.arange(len(table), dtype=jnp.int32)[None, :]
    piece = jnp.sum(jnp.where(chosen, jnp.asarray(table[:, 0])[None, :], 0), 1)
    place = jnp.sum(jnp.where(chosen, jnp.asarray(table[:, 1])[None, :], 0), 1)
    groups = (live + GROUP - 1) // GROUP
    number = jnp.arange(slots, dtype=jnp.int32)
    key = jnp.where(number < groups * GROUP, piece, pieces)
    key = key * slots + number
    rank = jnp.sum((key[None, :] < key[:, None]).astype(jnp.int32), 1)
    order = jnp.sum(jnp.where(rank[None, :] == number[:, None], number[None, :], 0), 1)
    limits = jnp.arange(pieces + 1, dtype=jnp.int32) * slots
    starts = jnp.sum((key[None, :] < limits[:, None]).astype(jnp.int32), 1)
    return order, starts, place, groups


def half_sum_kernel(keep, received, coded):
    blocks, side = keep.shape[:2]
    scales = decode_scales(received.at[0], side, blocks)
    which = lax.broadcasted_iota(jnp.int32, scales.shape, 0)

    def tile(t):
        scale = jnp.sum(jnp.where(which == t, scales, 0.0), axis=0, keepdims=True)
        rows = received[0, pl.ds(pl.multiple_of(t * side, side), side), :]
        return keep[t] + rows.astype(jnp.int32).astype(jnp.float32) * scale

    encode_block(tile, coded, side, blocks)


def half_sum(keep, received, which):
    blocks, side, width = keep.shape
    length = received.shape[1]
    return pl.pallas_call(
        half_sum_kernel,
        out_shape=jax.ShapeDtypeStruct((length, width), jnp.int16),
        grid=(1,),
        in_specs=[
            pl.BlockSpec((blocks, side, width), lambda i: (0, 0, 0)),
            pl.BlockSpec((1, length, width), lambda i: (which, 0, 0)),
        ],
        out_specs=pl.BlockSpec((length, width), lambda i: (0, 0)),
        compiler_params=pltpu.CompilerParams(vmem_limit_bytes=SMALL_VMEM),
        cost_estimate=pl.CostEstimate(flops=1 << 22, bytes_accessed=2 << 20, transcendentals=0),
        name="half_sum",
    )(keep, received)


def total_kernel(keep, received, first, second, third, sampled, gram):
    blocks, side = keep.shape[:2]
    parts = [received.at[0], first, second, third]
    scales = [decode_scales(p, side, blocks) for p in parts]
    which = lax.broadcasted_iota(jnp.int32, scales[0].shape, 0)

    def tile(t, _):
        rows = pl.ds(pl.multiple_of(t * side, side), side)
        terms = [keep[t]]
        for p, s in zip(parts, scales):
            scale = jnp.sum(jnp.where(which == t, s, 0.0), axis=0, keepdims=True)
            terms.append(p[rows, :].astype(jnp.int32).astype(jnp.float32) * scale)
        sampled[rows, :] = (terms[0] + terms[1]) + (terms[2] + terms[3]) + terms[4]
        return 0

    lax.fori_loop(0, blocks, tile, 0)
    piece = 4 * side
    acc = None
    for i in range(blocks // 4):
        part = sampled[pl.ds(i * piece, piece), :]
        term = lax.dot_general(
            part, part, (((0,), (0,)), ((), ())), precision=HIGHEST, preferred_element_type=jnp.float32
        )
        acc = term if acc is None else acc + term
    gram[...] = acc


def total_sum(keep, received, which, others):
    blocks, side, width = keep.shape
    length = received.shape[1]
    whole = pl.BlockSpec((length, width), lambda i: (0, 0))
    return pl.pallas_call(
        total_kernel,
        out_shape=(
            jax.ShapeDtypeStruct((blocks * side, width), jnp.float32),
            jax.ShapeDtypeStruct((width, width), jnp.float32),
        ),
        grid=(1,),
        in_specs=[
            pl.BlockSpec((blocks, side, width), lambda i: (0, 0, 0)),
            pl.BlockSpec((1, length, width), lambda i: (which, 0, 0)),
            whole,
            whole,
            whole,
        ],
        out_specs=(
            pl.BlockSpec((blocks * side, width), lambda i: (0, 0)),
            pl.BlockSpec((width, width), lambda i: (0, 0)),
        ),
        compiler_params=pltpu.CompilerParams(vmem_limit_bytes=SMALL_VMEM),
        name="total_sum",
    )(keep, received, *others)


def finish_kernel(order, gram, sampled, basis, factor, work):
    n = gram.shape[0]
    row = lax.broadcasted_iota(jnp.int32, (n, n), 0)
    column = lax.broadcasted_iota(jnp.int32, (n, n), 1)
    work[:, :n] = gram[...] * (1.0 / order)
    work[:, n:] = jnp.where(row == column, 1.0, 0.0)
    inside = lax.broadcasted_iota(jnp.int32, (PANEL, 1), 0)
    for base in range(0, n, PANEL):
        end = base + PANEL
        part = work[base:end, :]
        pivots = jnp.zeros((PANEL, 1), jnp.float32)
        for j in range(PANEL):
            pivot_row = part[j : j + 1, :]
            pivot = pivot_row[:, base + j : base + j + 1]
            pivots = jnp.where(inside == j, pivot, pivots)
            if j + 1 < PANEL:
                below = jnp.where(inside > j, part[:, base + j : base + j + 1] * (1.0 / pivot), 0.0)
                part = part - below * pivot_row
        part = part * (1.0 / jnp.sqrt(pivots))
        work[base:end, :] = part
        if end < n:
            work[end:, :] -= lax.dot_general(
                part[:, end:n],
                part,
                (((0,), (0,)), ((), ())),
                precision=HIGHEST,
                preferred_element_type=jnp.float32,
            )
    factor[...] = jnp.where(column >= row, work[:, :n], 0.0)
    inverse = work[:, n:]
    piece = 4 * n
    for i in range(sampled.shape[0] // piece):
        rows = pl.ds(i * piece, piece)
        basis[rows, :] = lax.dot_general(
            sampled[rows, :],
            inverse,
            (((1,), (1,)), ((), ())),
            precision=HIGHEST,
            preferred_element_type=jnp.float32,
        )


def finish(order, gram, sampled):
    n = gram.shape[0]
    return pl.pallas_call(
        lambda *refs: finish_kernel(order, *refs),
        out_shape=(
            jax.ShapeDtypeStruct(sampled.shape, jnp.float32),
            jax.ShapeDtypeStruct(gram.shape, jnp.float32),
        ),
        scratch_shapes=[pltpu.VMEM((n, 2 * n), jnp.float32)],
        compiler_params=pltpu.CompilerParams(vmem_limit_bytes=SMALL_VMEM),
        name="finish",
    )(gram, sampled)


def swap(value, axes, mask, size):
    return lax.ppermute(value, axes, [(i, i ^ mask) for i in range(size)])


def sum_four(value, axes, low, high, size):
    others = [swap(value, axes, m, size) for m in (low, high, low ^ high)]
    return (value + others[0]) + (others[1] + others[2])


def shards(tiles, tile_row, tile_owner, tile_offset, counts, sketch):
    row_count = lax.axis_size("row")
    col_count = lax.axis_size("col")
    slot_count, side = tiles.shape[1:3]
    width = sketch.shape[1]
    blocks = sketch.shape[0] // side
    place = lax.axis_index("col")
    core, chip = place % 2, place // 2
    live = counts[0]
    omega, table, early = gather_rows(sketch, side)
    tile_row, tile_owner, tile_offset, _ = lax.optimization_barrier((tile_row, tile_owner, tile_offset, early))
    rows = jnp.where(jnp.arange(slot_count, dtype=jnp.int32) < live, tile_row[0], col_count * blocks)
    order, starts, where, groups = plan(tile_owner[0, :, 0], tile_offset[0], live, table, len(omega), blocks)
    distances = (2, 1, 3, 0)
    meta = jnp.stack([groups, core, *[chip ^ k for k in distances]]).astype(jnp.int32)
    *keep, send = products(
        tiles[0], omega, order, starts, where, rows, meta, col_count // 2, blocks
    )

    received = swap(send, "col", 1, col_count)
    others = []
    for i in range(3):
        coded = half_sum(keep[i], received, i)
        others.append(swap(coded, "col", 2 * distances[i], col_count))
    sampled, local_gram = total_sum(keep[3], received, 3, others)

    both = ("row", "col")
    devices = row_count * col_count
    gram = sum_four(local_gram, both, 1, 4 * col_count, devices)
    gram = sum_four(gram, both, 2, 4, devices)
    gram = sum_four(gram, both, col_count, 2 * col_count, devices)
    gram = sum_four(gram, both, 8 * col_count, 16 * col_count, devices)
    return finish(sampled.shape[0] * devices, gram, sampled)


def solution(mesh):
    in_specs = (
        P(("row", "col"), None, None, None),
        P(("row", "col"), None),
        P(("row", "col"), None, None),
        P(("row", "col"), None),
        P(("row", "col")),
        P(("col", "row"), None),
    )
    out_specs = (P(("row", "col"), None), P())
    return jax.shard_map(shards, mesh=mesh, in_specs=in_specs, out_specs=out_specs, check_vma=False)
```
